256 devices in a mesh: section: 8 (over x, core), tp: 4 (over z_lo), fsdp: 8 (over y, z_hi).
Axes of the slice: x: 4, y: 4, z: 8 (z_hi: 2, z_lo: 4; z = z_hi * 4 + z_lo), core: 2. Of those that a mesh axis runs over, the one named last changes fastest.
Arguments:
- teacher_updates: bfloat16 [8, 256, 4, 16384], P('section', 'fsdp', None, 'tp'), may hold values from -6 to 6
- layer_map: int32 [8, 32], replicated, may hold values from 0 to 7
- route: int32 [8, 32], replicated, may hold values from 0 to 7, as said below
- projector: bfloat16 [16384, 5120], P('tp', 'section'), may hold values from -0.046875 to 0.046875
- student_in: bfloat16 [8, 8, 16, 5120], P('fsdp'), may hold values from -6 to 6
- norm_gain: float32 [5120], replicated, may hold values from 0.25 to 1.75
- w_gate: bfloat16 [5120, 12800], P('fsdp', ('section', 'tp')), may hold values from -0.078125 to 0.078125
- w_up: bfloat16 [5120, 12800], P('fsdp', ('section', 'tp')), may hold values from -0.078125 to 0.078125
- w_down: bfloat16 [12800, 5120], P(('section', 'tp'), 'fsdp'), may hold values from -0.0546875 to 0.0546875
Outputs:
- gate_grad: float32 [5120, 12800], P('fsdp', ('section', 'tp'))
- up_grad: float32 [5120, 12800], P('fsdp', ('section', 'tp'))
- down_grad: float32 [12800, 5120], P(('section', 'tp'), 'fsdp')
The draws below stay inside these ranges and needn't reach their ends.
Inputs may be any that keep to these rules, and one draw needn't show every extreme that they name: Each row of route names every student shard exactly 4 times: every teacher column sends 4 micro-batches to each student shard.
All inputs are finite; a program needn't handle non-finite values.
Results may differ from the reference program's by a relative error of at most 0.023.
Values may be sent and summed in bfloat16 or wider, within the bound.
A program may use at most 128 MiB of HBM per device.

```python
import jax
import jax.numpy as jnp
from jax import lax

TEACHER_WIDTH = 16384
STUDENT_WIDTH = 5120
STUDENT_HIDDEN = 12800
ROWS = 4
SENDS = 4
LAYERS = 8
BATCHES = 256
N_SECTION = 8
N_TP = 4
N_FSDP = 8


def draw_route(key, part):
    key = jax.random.fold_in(key, 7919)
    row_keys = jax.random.split(key, N_FSDP)
    base = jnp.repeat(jnp.arange(N_FSDP, dtype=jnp.int32), SENDS)
    rows = jax.vmap(lambda k: jax.random.permutation(k, base))(row_keys)
    return rows.astype(jnp.int32)


def place_ends(entries, key, low, high):
    dims = entries.shape
    spot = [jax.random.randint(jax.random.fold_in(key, axis), (), 0, dims[axis]) for axis in range(len(dims))]
    entries = entries.at[tuple(spot)].set(low)
    longest = dims.index(max(dims))
    spot[longest] = (spot[longest] + 1) % dims[longest]
    return entries.at[tuple(spot)].set(high)


def block_scale(stream_key, shape, cuts, smallest, top_value):
    factor_of = 1.0
    for dim, parts in cuts:
        draws = jax.random.uniform(jax.random.fold_in(jax.random.fold_in(stream_key, 6), dim), (parts,), jnp.float32, smallest / len(cuts), top_value / len(cuts))
        factor_of = factor_of * jnp.repeat(jnp.exp(draws), shape[dim] // parts).reshape((-1,) + (1,) * (len(shape) - 1 - dim))
    return factor_of


def scatter_about(rng, extent, scale, most, cuts=(), kind=jnp.bfloat16):
    array = scale * jax.random.normal(rng, extent, jnp.float32)
    if cuts:
        array = array * block_scale(rng, extent, cuts, -0.22, 0.18)
    return jnp.clip(array, -most, most).astype(kind)


def setup_inputs(seed: int = 0) -> dict:
    splits = jax.random.split(jax.random.key(seed), 10)
    return {
        "teacher_updates": scatter_about(splits[0], (LAYERS, BATCHES, ROWS, TEACHER_WIDTH), 1.0, 6.0, ((0, 8), (1, 8), (3, 4))),
        "layer_map": place_ends(jax.random.randint(splits[1], (N_FSDP, N_FSDP * SENDS), 0, N_SECTION), jax.random.fold_in(splits[1], 1), 0, N_SECTION - 1).astype(jnp.int32),
        "route": draw_route(jax.random.fold_in(splits[9], 71), 0),
        "projector": scatter_about(splits[3], (TEACHER_WIDTH, STUDENT_WIDTH), TEACHER_WIDTH ** -0.5, 0.046875, ((0, 4), (1, 8))),
        "student_in": scatter_about(splits[4], (N_FSDP, N_FSDP, SENDS * ROWS, STUDENT_WIDTH), 1.0, 6.0, ((0, 8),)),
        "norm_gain": jnp.clip(1.0 + 0.15 * jax.random.normal(splits[5], (STUDENT_WIDTH,), jnp.float32), 0.25, 1.75),
        "w_gate": scatter_about(splits[6], (STUDENT_WIDTH, STUDENT_HIDDEN), STUDENT_WIDTH ** -0.5, 0.078125, ((0, 8), (1, 32))),
        "w_up": scatter_about(splits[7], (STUDENT_WIDTH, STUDENT_HIDDEN), STUDENT_WIDTH ** -0.5, 0.078125, ((0, 8), (1, 32))),
        "w_down": scatter_about(splits[8], (STUDENT_HIDDEN, STUDENT_WIDTH), STUDENT_HIDDEN ** -0.5, 0.0546875, ((0, 32), (1, 8))),
    }


EPS = 1e-05

def reference(teacher_updates, layer_map, route, projector, student_in, norm_gain, w_gate, w_up, w_down):
    columns = layer_map.shape[0]
    slots = layer_map.shape[1]
    repeats = slots // columns
    section_ids = jnp.arange(N_SECTION, dtype=jnp.int32)
    per_batch = jnp.swapaxes(teacher_updates, 0, 1)

    def pick_layer(operands):
        updates, layer = operands
        keep = (section_ids <= layer).astype(jnp.float32)
        return lax.optimization_barrier(jnp.sum(updates.astype(jnp.float32) * keep[:, None, None], axis=0)).astype(jnp.bfloat16)
    picked = lax.map(pick_layer, (per_batch, layer_map.reshape(-1)))

    def project(hidden_rows):
        values = hidden_rows.astype(jnp.float32)
        scale = lax.rsqrt(lax.optimization_barrier(jnp.mean(values * values, axis=1)) + EPS)
        return jnp.dot(hidden_rows, projector, preferred_element_type=jnp.float32) * scale[:, None]
    projected = lax.map(project, picked).reshape(columns, slots, ROWS, STUDENT_WIDTH)
    shard_ids = jnp.arange(columns, dtype=jnp.int32)
    matches = (route[:, :, None] == shard_ids[None, None, :]).astype(jnp.int32)
    ranks = lax.optimization_barrier(jnp.sum(jnp.cumsum(matches, axis=1) * matches, axis=2)) - 1
    rank_ids = jnp.arange(repeats, dtype=jnp.int32)
    selector = (matches[:, :, :, None] * (ranks[:, :, None, None] == rank_ids[None, None, None, :]).astype(jnp.int32)).astype(jnp.float32)
    aligned = jnp.einsum('jmdk,jmrc->djkrc', selector, projected, precision=lax.Precision.HIGHEST)
    target = aligned.reshape(-1, STUDENT_WIDTH)
    inputs = student_in.astype(jnp.float32).reshape(-1, STUDENT_WIDTH)
    inv_rms = lax.rsqrt(lax.optimization_barrier(jnp.mean(inputs * inputs, axis=1, keepdims=True)) + EPS)
    normed = (inputs * inv_rms * norm_gain).astype(jnp.bfloat16)
    pieces = N_SECTION * N_TP
    width = STUDENT_HIDDEN // pieces
    gate_parts = jnp.transpose(w_gate.reshape(STUDENT_WIDTH, pieces, width), (1, 0, 2))
    up_parts = jnp.transpose(w_up.reshape(STUDENT_WIDTH, pieces, width), (1, 0, 2))
    down_parts = w_down.reshape(pieces, width, STUDENT_WIDTH)

    def hidden_of(gate_weights, up_weights):
        gate_act = jnp.dot(normed, gate_weights, preferred_element_type=jnp.float32)
        up_act = jnp.dot(normed, up_weights, preferred_element_type=jnp.float32)
        return (gate_act, up_act, (jax.nn.silu(gate_act) * up_act).astype(jnp.bfloat16))

    def forward(total, weights):
        gate_weights, up_weights, down_weights = weights
        _, _, hidden = hidden_of(gate_weights, up_weights)
        product = jnp.dot(hidden, down_weights, preferred_element_type=jnp.float32).astype(jnp.bfloat16)
        product = lax.optimization_barrier(product)
        return (total + product.astype(jnp.float32), None)
    mixed, _ = lax.scan(forward, jnp.zeros(inputs.shape, jnp.float32), (gate_parts, up_parts, down_parts))
    error = inputs + mixed - target
    delta = (error / ROWS).astype(jnp.bfloat16)
    normed_by_shard = normed.reshape(columns, -1, STUDENT_WIDTH).astype(jnp.float32)
    delta_by_shard = delta.reshape(columns, -1, STUDENT_WIDTH).astype(jnp.float32)

    def shard_sum(partials):
        rounded = lax.optimization_barrier(partials.astype(jnp.bfloat16))
        return lax.optimization_barrier(jnp.sum(rounded.astype(jnp.float32), axis=0))

    def backward(carry, weights):
        gate_weights, up_weights, down_weights = weights
        gate_act, up_act, hidden = hidden_of(gate_weights, up_weights)
        d_hidden = lax.dot_general(delta, down_weights, (((1,), (1,)), ((), ())), preferred_element_type=jnp.float32)
        sig = jax.nn.sigmoid(gate_act)
        d_gate = (d_hidden * up_act * sig * (1.0 + gate_act * (1.0 - sig))).astype(jnp.bfloat16)
        d_up = (d_hidden * gate_act * sig).astype(jnp.bfloat16)
        gate_part = shard_sum(jnp.einsum('srk,srh->skh', normed_by_shard, d_gate.reshape(columns, -1, width).astype(jnp.float32)))
        up_part = shard_sum(jnp.einsum('srk,srh->skh', normed_by_shard, d_up.reshape(columns, -1, width).astype(jnp.float32)))
        down_part = shard_sum(jnp.einsum('srh,src->shc', hidden.reshape(columns, -1, width).astype(jnp.float32), delta_by_shard))
        return (carry, (gate_part, up_part, down_part))
    _, (gate_all, up_all, down_all) = lax.scan(backward, jnp.zeros((), jnp.float32), (gate_parts, up_parts, down_parts))
    gate_grad = jnp.transpose(gate_all, (1, 0, 2)).reshape(STUDENT_WIDTH, STUDENT_HIDDEN)
    up_grad = jnp.transpose(up_all, (1, 0, 2)).reshape(STUDENT_WIDTH, STUDENT_HIDDEN)
    down_grad = down_all.reshape(STUDENT_HIDDEN, STUDENT_WIDTH)
    return (gate_grad, up_grad, down_grad)
```

```python
import jax
import jax.numpy as jnp
from jax import lax
from jax.experimental import pallas as pl
from jax.experimental.pallas import tpu as pltpu
from jax.sharding import PartitionSpec as P

MESH = pl.DeviceIdType.MESH
EPS = 1e-05
F32 = jnp.float32
BF16 = jnp.bfloat16

TW = 4096
SW = 640
SUB = 80
HW = 400
TEACHER_WIDTH = 16384
STUDENT_WIDTH = 5120
ROWS = 4

NN = (((1,), (0,)), ((), ()))
NT = (((1,), (1,)), ((), ()))
TN = (((0,), (0,)), ((), ()))


def dot(a, b, dims):
    return lax.dot_general(a, b, dims, preferred_element_type=F32)


SCRATCH = (
    ("u", (8, 16, TW), BF16),
    ("t1r", (8, 16, TW), BF16),
    ("pk", (8, 16, TW), BF16),
    ("prs", (4, 32, SW + 256), BF16),
    ("t3r", (3, 32, SW + 256), BF16),
    ("t4s", (32, SW), F32),
    ("t4r", (32, SW), F32),
    ("xr", (2, 16, SW), BF16),
    ("a1s", (8, SUB, 128), BF16),
    ("nt", (8, 8, SUB, 128), BF16),
    ("g1", (4, 2, 2 * HW, 128), BF16),
    ("gr", (3, 2, 2 * HW, 128), BF16),
    ("gzs", (2 * HW, 128), BF16),
    ("gzr", (2 * HW, 128), BF16),
    ("a1", (HW, 128), F32),
    ("a2", (HW, 128), F32),
    ("ht", (4, 2, HW, 128), BF16),
    ("pb", (8, 4, 2, 16, SW), BF16),
    ("d1r", (8, 4, 16, SW), BF16),
    ("q", (8, 4, 16, SW), BF16),
    ("d2r", (3, 8, 16, SW), BF16),
    ("r", (4, 2, 16, SW), BF16),
    ("d3r", (3, 2, 16, SW), BF16),
    ("dl", (8, 8, 16, SW), BF16),
    ("h1", (4, 2, HW, 128), BF16),
    ("hr", (3, 2, HW, 128), BF16),
    ("hzs", (HW, 128), BF16),
    ("hzr", (HW, 128), BF16),
    ("dg", (4, 2, 2 * HW, 128), BF16),
)
N_SEM = 96


class Refs:
    pass


def kernel(upd, perm, proj, xin, gsub, wg, wu, wd, gate_o, up_o, down_o, *scratch):
    b = Refs()
    for (name, _, _), ref in zip(SCRATCH, scratch):
        setattr(b, name, ref)
    send_sem, recv_sem = scratch[len(SCRATCH) :]
    s = lax.axis_index("section")
    t = lax.axis_index("tp")
    f = lax.axis_index("fsdp")
    x, core = s // 2, s % 2
    y, zh = f // 2, f % 2
    used = [2]
    started = []

    def describe(src, dst, dev, sem=None):
        if sem is None:
            sem = used[0]
            used[0] += 1
        return pltpu.make_async_remote_copy(
            src_ref=src,
            dst_ref=dst,
            send_sem=send_sem.at[sem],
            recv_sem=recv_sem.at[sem],
            device_id=dev,
            device_id_type=MESH,
        )

    def send(src, dst, dev):
        copy = describe(src, dst, dev)
        copy.start()
        started.append(copy)
        return copy

    def on_x(o):
        return {"section": (x + o) % 4 * 2 + core}

    def on_y(o):
        return {"fsdp": (y + o) % 4 * 2 + zh}

    def on_tp(o):
        return {"tp": (t + o) % 4}

    other_core = {"section": x * 2 + 1 - core}
    other_z = {"fsdp": y * 2 + 1 - zh}
    swapped = {"section": f, "fsdp": s}

    barrier = pltpu.get_barrier_semaphore()
    for o in range(1, 8):
        pl.semaphore_signal(barrier, inc=1, device_id={"section": (s + o) % 8}, device_id_type=MESH)
        pl.semaphore_signal(barrier, inc=1, device_id={"fsdp": (f + o) % 8}, device_id_type=MESH)
    for o in range(1, 4):
        pl.semaphore_signal(barrier, inc=1, device_id=on_tp(o), device_id_type=MESH)

    @pl.when(s != f)
    def _():
        pl.semaphore_signal(barrier, inc=1, device_id=swapped, device_id_type=MESH)

    total = jnp.zeros((128, 1), F32)
    for k in range(8):
        v = xin[:, :, k * SW : (k + 1) * SW].reshape(128, SW).astype(F32)
        total = total + jnp.sum(v * v, axis=1, keepdims=True)
    inv = lax.rsqrt(total / STUDENT_WIDTH + EPS)
    inv = jnp.broadcast_to(inv, (128, 128)).T[0:1, :]
    rows = lax.broadcasted_iota(jnp.int32, (SUB, SW), 0)
    cols = lax.broadcasted_iota(jnp.int32, (SUB, SW), 1)
    sel = jnp.where(cols == rows + s * SUB, 1.0, 0.0).astype(BF16)
    for k in range(8):
        xt = dot(sel, xin[:, :, k * SW : (k + 1) * SW].reshape(128, SW), NT)
        b.a1s[k] = (xt * inv * gsub[k]).astype(BF16)

    pl.semaphore_wait(barrier, jnp.where(s == f, 17, 18))

    a1 = []
    for o in range(1, 8):
        k = (f + o) % 8
        a1.append(send(b.a1s.at[k], b.nt.at[f, s], {"fsdp": k}))
    b.nt[f, s] = b.a1s[f]

    for k in range(4):
        cut = slice(k * (TW // 4), (k + 1) * (TW // 4))
        b.u[:, :, cut] = dot(perm[...], upd[:, cut], NN).astype(BF16).reshape(8, 16, TW // 4)
    t1 = []
    for o in range(1, 8):
        k = (s + o) % 8
        t1.append(send(b.u.at[k], b.t1r.at[s], {"section": k}))

    xsends = []
    for o in range(1, 8):
        k = (f + o) % 8
        c = pltpu.make_async_remote_copy(
            src_ref=xin.at[s, :, pl.ds(pl.multiple_of(k * SW, 128), SW)],
            dst_ref=b.xr.at[zh],
            send_sem=send_sem.at[used[0]],
            recv_sem=recv_sem.at[zh],
            device_id={"fsdp": k},
            device_id_type=MESH,
        )
        used[0] += 1
        xsends.append(c)

    @pl.when(y == t)
    def _():
        for c in xsends:
            c.start()
        b.xr[zh] = xin[s, :, pl.ds(pl.multiple_of(f * SW, 128), SW)]

    def spread_start(at):
        copies = [send(at(s), at(s), on_x(o)) for o in range(1, 4)]
        across = [send(at(s), at(s), other_core)]
        return at, copies, across

    def spread_forward(state):
        at, copies, across = state
        for o in range(1, 4):
            copies[o - 1].wait_recv()
            k = (x - o + 4) % 4 * 2 + core
            across.append(send(at(k), at(k), other_core))

    def spread_end(state):
        for c in state[2]:
            c.wait_recv()

    for c in a1:
        c.wait_recv()
    a2 = spread_start(lambda k: b.nt.at[:, k])

    for c in t1:
        c.wait_recv()
    for k in range(4):
        cut = slice(k * (TW // 4), (k + 1) * (TW // 4))
        acc = b.u[s, :, cut].astype(F32)
        for o in range(1, 8):
            acc = acc + b.t1r[(s + o) % 8, :, cut].astype(F32)
        b.pk[s, :, cut] = acc.astype(BF16)
    t2 = spread_start(lambda k: b.pk.at[k])

    spread_forward(a2)
    spread_end(a2)

    def reduce_start(src, got, product):
        copies = []
        for o in (1, 2, 3, 0):
            k = (y + o) % 4
            r = product(k)
            src[k, 0] = r[:, :128].astype(BF16)
            src[k, 1] = r[:, 128:].astype(BF16)
            if o:
                copies.append(send(src.at[k], got.at[o - 1], on_y(o)))
        return copies

    def reduce_across(copies, src, got, zs, zr, height):
        for c in copies:
            c.wait_recv()
        for k in range(0, height, HW // 5):
            cut = slice(k, k + HW // 5)
            acc = src[y, 1 - zh, cut].astype(F32)
            for o in range(3):
                acc = acc + got[o, 1 - zh, cut].astype(F32)
            zs[cut] = acc.astype(BF16)
        return send(zs, zr, other_z)

    def reduced(src, got, zr, cut):
        acc = src[y, zh, cut].astype(F32)
        for o in range(3):
            acc = acc + got[o, zh, cut].astype(F32)
        return acc + zr[cut].astype(F32)

    def gather_start(buf):
        own = buf.at[y, zh]
        far = send(own, own, other_z)
        return buf, far, [send(own, own, on_y(o)) for o in range(1, 4)]

    def gather_end(state):
        buf, far, copies = state
        far.wait_recv()
        copies += [send(buf.at[y, 1 - zh], buf.at[y, 1 - zh], on_y(o)) for o in range(1, 4)]
        for c in copies:
            c.wait_recv()

    def gate_up(k):
        pair = jnp.concatenate([b.nt[2 * k].reshape(SW, 128), b.nt[2 * k + 1].reshape(SW, 128)], axis=1)
        return jnp.concatenate([dot(wg[...], pair, NN), dot(wu[...], pair, NN)], axis=0)

    copies = reduce_start(b.g1, b.gr, gate_up)
    spread_forward(t2)
    far = reduce_across(copies, b.g1, b.gr, b.gzs, b.gzr, 2 * HW)

    spread_end(t2)
    squares = jnp.zeros((128, 1), F32)
    for k in range(4):
        v = b.pk[:, :, k * (TW // 4) : (k + 1) * (TW // 4)].reshape(128, TW // 4).astype(F32)
        squares = squares + jnp.sum(v * v, axis=1, keepdims=True)
    squares = jnp.broadcast_to(squares, (128, 128))
    high = squares.astype(BF16)
    b.prs[:, :, SW : SW + 128] = high.reshape(4, 32, 128)
    b.prs[:, :, SW + 128 :] = (squares - high.astype(F32)).astype(BF16).reshape(4, 32, 128)
    b.prs[:, :, :SW] = dot(b.pk[...].reshape(128, TW), proj[...], NN).astype(BF16).reshape(4, 32, SW)
    t3 = [send(b.prs.at[(t + o) % 4], b.t3r.at[o - 1], on_tp(o)) for o in range(1, 4)]

    far.wait_recv()
    for k in range(0, HW, HW // 5):
        cut = slice(k, k + HW // 5)
        gate = reduced(b.g1, b.gr, b.gzr, cut)
        up = reduced(b.g1, b.gr, b.gzr, slice(HW + k, HW + k + HW // 5))
        sig = 1.0 / (1.0 + jnp.exp(-gate))
        b.ht[y, zh, cut] = (gate * sig * up).astype(BF16)
        b.a1[cut] = up * sig * (1.0 + gate * (1.0 - sig))
        b.a2[cut] = gate * sig
    gather = gather_start(b.ht)

    for c in t3:
        c.wait_recv()
    acc = b.prs[t].astype(F32)
    for o in range(3):
        acc = acc + b.t3r[o].astype(F32)
    squares = acc[:, SW : SW + 1] + acc[:, SW + 128 : SW + 129]
    b.t4s[...] = acc[:, :SW] * lax.rsqrt(squares / TEACHER_WIDTH + EPS)
    t4 = describe(b.t4s, b.t4r, swapped)

    @pl.when(s != f)
    def _():
        t4.start()

    @pl.when(s == f)
    def _():
        b.t4r[...] = b.t4s[...]

    gather_end(gather)

    for k in range(8):
        r = dot(b.ht[k // 2, k % 2], wd[...], TN)
        b.pb[k] = r.astype(BF16).reshape(4, 2, 16, SW)
    d1 = send(b.pb.at[:, :, 1 - core], b.d1r, other_core)
    d1.wait_recv()
    for k in range(8):
        b.q[k] = (b.pb[k, :, core].astype(F32) + b.d1r[k].astype(F32)).astype(BF16)
    d2 = [send(b.q.at[:, (x + o) % 4], b.d2r.at[o - 1], on_x(o)) for o in range(1, 4)]
    for c in d2:
        c.wait_recv()
    for k in range(8):
        acc = b.q[k, x].astype(F32)
        for o in range(3):
            acc = acc + b.d2r[o, k].astype(F32)
        b.r[k // 2, k % 2] = acc.astype(BF16)
    d3 = [send(b.r.at[(t + o) % 4], b.d3r.at[o - 1], on_tp(o)) for o in range(1, 4)]

    @pl.when(s != f)
    def _():
        t4.wait_recv()

    for e in range(2):

        @pl.when(f != 2 * t + e)
        def _():
            describe(b.xr.at[e], b.xr.at[e], {"fsdp": (f + 1) % 8}, e).wait_recv()

    for c in d3:
        c.wait_recv()
    for e in range(2):
        acc = b.r[t, e].astype(F32)
        for o in range(3):
            acc = acc + b.d3r[o, e].astype(F32)
        error = b.xr[e].astype(F32) + acc - b.t4r[e * 16 : (e + 1) * 16]
        b.dl[2 * t + e, s] = (error / ROWS).astype(BF16)

    own = b.dl.at[pl.ds(2 * t, 2), s]
    for c in [send(own, own, on_tp(o)) for o in range(1, 4)]:
        c.wait_recv()
    e2 = spread_start(lambda k: b.dl.at[:, k])
    spread_forward(e2)
    spread_end(e2)

    def d_hidden(k):
        pair = jnp.concatenate([b.dl[2 * k].reshape(128, SW), b.dl[2 * k + 1].reshape(128, SW)], axis=0)
        return dot(wd[...], pair, NT)

    copies = reduce_start(b.h1, b.hr, d_hidden)
    hidden = jnp.concatenate([b.ht[k // 2, k % 2] for k in range(8)], axis=1)
    down_o[...] = dot(hidden, b.dl[...].reshape(1024, SW), NN)
    far = reduce_across(copies, b.h1, b.hr, b.hzs, b.hzr, HW)
    far.wait_recv()
    for k in range(0, HW, HW // 5):
        cut = slice(k, k + HW // 5)
        dh = reduced(b.h1, b.hr, b.hzr, cut)
        b.dg[y, zh, cut] = (dh * b.a1[cut]).astype(BF16)
        b.dg[y, zh, HW + k : HW + k + HW // 5] = (dh * b.a2[cut]).astype(BF16)
    gather_end(gather_start(b.dg))

    normed = jnp.concatenate([b.nt[k].reshape(SW, 128) for k in range(8)], axis=1)
    d_gate = jnp.concatenate([b.dg[k // 2, k % 2, 0:HW] for k in range(8)], axis=1)
    gate_o[...] = dot(d_gate, normed, NT)
    d_up = jnp.concatenate([b.dg[k // 2, k % 2, HW : 2 * HW] for k in range(8)], axis=1)
    up_o[...] = dot(d_up, normed, NT)

    for c in started:
        c.wait_send()

    @pl.when(s != f)
    def _():
        t4.wait_send()

    @pl.when(y == t)
    def _():
        for c in xsends:
            c.wait_send()


def on_device(
    teacher_updates, layer_map, route, projector, student_in, norm_gain, w_gate, w_up, w_down
):
    section = lax.axis_index("section")
    column = lax.axis_index("fsdp")
    layers = lax.dynamic_index_in_dim(layer_map, column, 0, keepdims=False)
    dest = lax.dynamic_index_in_dim(route, column, 0, keepdims=False)
    slots = jnp.arange(32, dtype=jnp.int32)
    before = (dest[:, None] == dest[None, :]) & (slots[:, None] < slots[None, :])
    rank = jnp.sum(before.astype(jnp.int32), axis=0)
    place = jnp.where(layers >= section, dest * 4 + rank, -1)
    token = jnp.arange(128, dtype=jnp.int32)
    wanted = (place[:, None] * 4 + jnp.arange(4, dtype=jnp.int32)[None, :]).reshape(128)
    perm = (token[:, None] == wanted[None, :]).astype(BF16)
    gain = lax.dynamic_index_in_dim(norm_gain.reshape(8, 8, SUB), section, 1, keepdims=False)
    gain = jnp.broadcast_to(gain[:, :, None], (8, SUB, 128))

    vmem = pl.BlockSpec(memory_space=pltpu.VMEM)
    gate_grad, up_grad, down_grad = pl.pallas_call(
        kernel,
        out_shape=(
            jax.ShapeDtypeStruct((HW, SW), F32),
            jax.ShapeDtypeStruct((HW, SW), F32),
            jax.ShapeDtypeStruct((HW, SW), F32),
        ),
        in_specs=[vmem] * 8,
        out_specs=(vmem,) * 3,
        scratch_shapes=[pltpu.VMEM(shape, kind) for _, shape, kind in SCRATCH]
        + [pltpu.SemaphoreType.DMA((N_SEM,)), pltpu.SemaphoreType.DMA((N_SEM,))],
        compiler_params=pltpu.CompilerParams(
            collective_id=0, has_side_effects=True, vmem_limit_bytes=56 * 1024 * 1024
        ),
    )(
        teacher_updates.reshape(128, TW),
        perm,
        projector,
        student_in.reshape(8, 16, STUDENT_WIDTH),
        gain,
        w_gate.T,
        w_up.T,
        w_down,
    )
    return gate_grad.T, up_grad.T, down_grad


def solution(mesh):
    placed = (
        P("section", "fsdp", None, "tp"),
        P(),
        P(),
        P("tp", "section"),
        P("fsdp", None, None, None),
        P(),
        P("fsdp", ("section", "tp")),
        P("fsdp", ("section", "tp")),
        P(("section", "tp"), "fsdp"),
    )
    return jax.shard_map(
        on_device,
        mesh=mesh,
        in_specs=placed,
        out_specs=(
            P("fsdp", ("section", "tp")),
            P("fsdp", ("section", "tp")),
            P(("section", "tp"), "fsdp"),
        ),
        check_vma=False,
    )
```

```python
import jax
import jax.numpy as jnp
from jax import lax
from jax.experimental import pallas as pl
from jax.experimental.pallas import tpu as pltpu
from jax.sharding import PartitionSpec as P

MESH = pl.DeviceIdType.MESH
EPS = 1e-05
F32 = jnp.float32
BF16 = jnp.bfloat16

TW = 4096
SW = 640
SUB = 80
HW = 400
TEACHER_WIDTH = 16384
STUDENT_WIDTH = 5120
ROWS = 4

NN = (((1,), (0,)), ((), ()))
NT = (((1,), (1,)), ((), ()))
TN = (((0,), (0,)), ((), ()))


def dot(a, b, dims):
    return lax.dot_general(a, b, dims, preferred_element_type=F32)


SCRATCH = (
    ("updv", (32, 4, TW), BF16),
    ("projv", (TW, SW), BF16),
    ("wg", (HW, SW), BF16),
    ("wu", (HW, SW), BF16),
    ("wd", (HW, SW), BF16),
    ("u", (8, 16, TW), BF16),
    ("t1r", (8, 16, TW), BF16),
    ("pk", (8, 16, TW), BF16),
    ("prs", (4, 32, SW + 256), BF16),
    ("t3r", (3, 32, SW + 256), BF16),
    ("t4s", (32, SW), F32),
    ("t4r", (32, SW), F32),
    ("xr", (2, 16, SW), BF16),
    ("a1s", (8, SUB, 128), BF16),
    ("nt", (4, 2, 8, SUB, 128), BF16),
    ("g1", (2, 4, 2 * HW, 128), BF16),
    ("gr", (2, 3, 2 * HW, 128), BF16),
    ("gzs", (2 * HW, 128), BF16),
    ("gzr", (2 * HW, 128), BF16),
    ("aa", (4, 2, 2 * HW, 128), BF16),
    ("ht", (4, 2, HW, 128), BF16),
    ("pb", (8, 4, 2, 16, SW), BF16),
    ("d1r", (8, 4, 16, SW), BF16),
    ("q", (8, 4, 16, SW), BF16),
    ("d2r", (3, 8, 16, SW), BF16),
    ("r", (4, 2, 16, SW), BF16),
    ("d3r", (3, 2, 16, SW), BF16),
    ("dl", (8, 8, 16, SW), BF16),
    ("h1", (2, 4, HW, 128), BF16),
    ("hr", (2, 3, HW, 128), BF16),
    ("hzs", (HW, 128), BF16),
    ("hzr", (HW, 128), BF16),
    ("dh", (4, 2, HW, 128), BF16),
)
N_SEM = 112
OUTS = ("nt", "ht", "dl", "aa", "dh")
CHUNK = HW // 5


class Refs:
    pass


def selection(layer_map, route, f, s):
    lane = lax.broadcasted_iota(jnp.int32, (32, 128), 1)
    slot = lax.broadcasted_iota(jnp.int32, (32, 128), 0)
    widen = jnp.where(lane // ROWS == slot, 1.0, 0.0).astype(BF16)
    mine = lax.broadcasted_iota(jnp.int32, (8, 128), 0) == f

    def row(table):
        wide = dot(table[...].astype(F32).astype(BF16), widen, NN)
        return jnp.sum(jnp.where(mine, wide, 0.0), axis=0, keepdims=True)

    dest, layer = row(route), row(layer_map)
    across = jnp.broadcast_to(dest, (128, 128))
    a = lax.broadcasted_iota(jnp.int32, (128, 128), 0)
    c = lax.broadcasted_iota(jnp.int32, (128, 128), 1)
    earlier = (across.T == across) & (a // ROWS < c // ROWS) & (a % ROWS == 0)
    rank = jnp.sum(jnp.where(earlier, 1.0, 0.0), axis=0, keepdims=True)
    place = (dest * 4.0 + rank) * ROWS + (c[0:1] % ROWS).astype(F32)
    place = jnp.where(layer >= s.astype(F32), place, -1.0)
    return jnp.where(a.astype(F32) == place, 1.0, 0.0).astype(BF16)


def kernel(upd, layer_map, route, proj, xin, gain, wg, wu, wd, *rest):
    outs, scratch = rest[: len(OUTS)], rest[len(OUTS) :]
    b = Refs()
    for (name, _, _), ref in zip(SCRATCH, scratch):
        setattr(b, name, ref)
    send_sem, recv_sem, in_sem, out_sem = scratch[len(SCRATCH) :]
    s = lax.axis_index("section")
    t = lax.axis_index("tp")
    f = lax.axis_index("fsdp")
    x, core = s // 2, s % 2
    y, zh = f // 2, f % 2
    far_z = 1 - zh
    used = [2]
    started = []

    def describe(src, dst, dev, sem=None):
        if sem is None:
            sem = used[0]
            used[0] += 1
        return pltpu.make_async_remote_copy(
            src_ref=src,
            dst_ref=dst,
            send_sem=send_sem.at[sem],
            recv_sem=recv_sem.at[sem],
            device_id=dev,
            device_id_type=MESH,
        )

    def send(src, dst, dev):
        copy = describe(src, dst, dev)
        copy.start()
        started.append(copy)
        return copy

    def on_x(o):
        return {"section": (x + o) % 4 * 2 + core}

    def on_y(o):
        return {"fsdp": (y + o) % 4 * 2 + zh}

    def on_tp(o):
        return {"tp": (t + o) % 4}

    other_core = {"section": x * 2 + 1 - core}
    other_z = {"fsdp": y * 2 + far_z}
    swapped = {"section": f, "fsdp": s}

    barrier = pltpu.get_barrier_semaphore()
    for o in range(1, 8):
        pl.semaphore_signal(barrier, inc=1, device_id={"section": (s + o) % 8}, device_id_type=MESH)
        pl.semaphore_signal(barrier, inc=1, device_id={"fsdp": (f + o) % 8}, device_id_type=MESH)
    for o in range(1, 4):
        pl.semaphore_signal(barrier, inc=1, device_id=on_tp(o), device_id_type=MESH)

    @pl.when(s != f)
    def _():
        pl.semaphore_signal(barrier, inc=1, device_id=swapped, device_id_type=MESH)

    loads = {}
    for k, (name, src, dst) in enumerate(
        (("wg", wg, b.wg), ("wu", wu, b.wu), ("upd", upd, b.updv), ("proj", proj, b.projv), ("wd", wd, b.wd))
    ):
        loads[name] = pltpu.make_async_copy(src, dst, in_sem.at[k])
        loads[name].start()

    def student(k):
        return xin[:, :, k * SW : (k + 1) * SW].reshape(128, SW).astype(F32)

    total = jnp.zeros((128, 1), F32)
    for k in range(8):
        v = student(k)
        total = total + jnp.sum(v * v, axis=1, keepdims=True)
    inv = lax.rsqrt(total / STUDENT_WIDTH + EPS)
    rows = lax.broadcasted_iota(jnp.int32, (SUB, SW), 0)
    cols = lax.broadcasted_iota(jnp.int32, (SUB, SW), 1)
    sel = jnp.where(cols == rows + s * SUB, 1.0, 0.0).astype(BF16)
    for k in range(8):
        normed = (student(k) * inv * gain[:, k * SW : (k + 1) * SW]).astype(BF16)
        b.a1s[k] = dot(sel, normed, NT).astype(BF16)

    pl.semaphore_wait(barrier, jnp.where(s == f, 17, 18))

    a1 = {}
    for dz, dy in ((1, 0), (1, 1), (1, 3), (1, 2), (0, 1), (0, 3), (0, 2)):
        k = (y + dy) % 4 * 2 + (zh + dz) % 2
        a1[dz, dy] = send(b.a1s.at[k], b.nt.at[y, zh, s], {"fsdp": k})
    b.nt[y, zh, s] = b.a1s[f]

    xsends = []
    for o in range(1, 8):
        k = (f + o) % 8
        c = pltpu.make_async_remote_copy(
            src_ref=xin.at[s, :, pl.ds(pl.multiple_of(k * SW, 128), SW)],
            dst_ref=b.xr.at[zh],
            send_sem=send_sem.at[used[0]],
            recv_sem=recv_sem.at[zh],
            device_id={"fsdp": k},
            device_id_type=MESH,
        )
        used[0] += 1
        xsends.append(c)

    @pl.when(y == t)
    def _():
        for c in xsends:
            c.start()
        b.xr[zh] = xin[s, :, pl.ds(pl.multiple_of(f * SW, 128), SW)]

    def spread_start(at):
        copies = [send(at(s), at(s), on_x(o)) for o in range(1, 4)]
        across = [send(at(s), at(s), other_core)]
        return at, copies, across

    def spread_forward(state):
        at, copies, across = state
        for o in range(1, 4):
            copies[o - 1].wait_recv()
            k = (x - o + 4) % 4 * 2 + core
            across.append(send(at(k), at(k), other_core))

    def spread_end(state):
        for c in state[2]:
            c.wait_recv()

    for dy in (1, 2, 3):
        a1[0, dy].wait_recv()
    near = spread_start(lambda k: b.nt.at[:, zh, k])

    perm = selection(layer_map, route, f, s)
    loads["upd"].wait()
    for k in range(4):
        cut = slice(k * (TW // 4), (k + 1) * (TW // 4))
        part = b.updv[:, :, cut].reshape(128, TW // 4)
        b.u[:, :, cut] = dot(perm, part, NN).astype(BF16).reshape(8, 16, TW // 4)

    for dy in (0, 1, 2, 3):
        a1[1, dy].wait_recv()
    far = spread_start(lambda k: b.nt.at[:, far_z, k])
    spread_forward(near)
    spread_forward(far)
    t1 = []
    for o in range(1, 8):
        k = (s + o) % 8
        t1.append(send(b.u.at[k], b.t1r.at[s], {"section": k}))
    loads["wg"].wait()
    loads["wu"].wait()
    spread_end(near)
    spread_end(far)

    def reduce_start(src, got, product):
        copies = []
        for h, z in ((0, far_z), (1, zh)):
            r = product(z)
            for k in range(4):
                src[h, k] = r[:, 128 * k : 128 * (k + 1)].astype(BF16)
            copies.append([send(src.at[h, (y + o) % 4], got.at[h, o - 1], on_y(o)) for o in (2, 1, 3)])
        return copies

    def partial_sum(src, got, h, cut):
        acc = src[h, y, cut].astype(F32)
        for o in range(3):
            acc = acc + got[h, o, cut].astype(F32)
        return acc

    def reduce_across(copies, src, got, zs, zr, height):
        for c in copies[0]:
            c.wait_recv()
        for k in range(0, height, CHUNK):
            cut = slice(k, k + CHUNK)
            zs[cut] = partial_sum(src, got, 0, cut).astype(BF16)
        return send(zs, zr, other_z)

    def gather_start(buf):
        own = buf.at[y, zh]
        far = send(own, own, other_z)
        return buf, far, [send(own, own, on_y(o)) for o in (2, 1, 3)]

    def gather_forward(state):
        buf, far, copies = state
        far.wait_recv()
        copies += [send(buf.at[y, far_z], buf.at[y, far_z], on_y(o)) for o in (2, 1, 3)]

    def gather_end(state):
        for c in state[2]:
            c.wait_recv()

    def gate_up(z):
        four = jnp.concatenate([b.nt[k, z].reshape(SW, 128) for k in range(4)], axis=1)
        return jnp.concatenate([dot(b.wg[...], four, NN), dot(b.wu[...], four, NN)], axis=0)

    copies = reduce_start(b.g1, b.gr, gate_up)
    stores = [pltpu.make_async_copy(b.nt, outs[0], out_sem.at[0])]
    stores[0].start()

    for c in t1:
        c.wait_recv()
    for k in range(4):
        cut = slice(k * (TW // 4), (k + 1) * (TW // 4))
        acc = b.u[s, :, cut].astype(F32)
        for o in range(1, 8):
            acc = acc + b.t1r[(s + o) % 8, :, cut].astype(F32)
        b.pk[s, :, cut] = acc.astype(BF16)
    t2 = spread_start(lambda k: b.pk.at[k])

    across = reduce_across(copies, b.g1, b.gr, b.gzs, b.gzr, 2 * HW)
    spread_forward(t2)
    for c in copies[1]:
        c.wait_recv()
    across.wait_recv()
    for k in range(0, HW, CHUNK):
        cut, low = slice(k, k + CHUNK), slice(HW + k, HW + k + CHUNK)
        gate = partial_sum(b.g1, b.gr, 1, cut) + b.gzr[cut].astype(F32)
        up = partial_sum(b.g1, b.gr, 1, low) + b.gzr[low].astype(F32)
        sig = 1.0 / (1.0 + jnp.exp(-gate))
        b.ht[y, zh, cut] = (gate * sig * up).astype(BF16)
        b.aa[y, zh, cut] = (up * sig * (1.0 + gate * (1.0 - sig))).astype(BF16)
        b.aa[y, zh, low] = (gate * sig).astype(BF16)
    hidden = gather_start(b.ht)

    spread_end(t2)
    squares = jnp.zeros((128, 1), F32)
    for k in range(4):
        v = b.pk[:, :, k * (TW // 4) : (k + 1) * (TW // 4)].reshape(128, TW // 4).astype(F32)
        squares = squares + jnp.sum(v * v, axis=1, keepdims=True)
    squares = jnp.broadcast_to(squares, (128, 128))
    high = squares.astype(BF16)
    b.prs[:, :, SW : SW + 128] = high.reshape(4, 32, 128)
    b.prs[:, :, SW + 128 :] = (squares - high.astype(F32)).astype(BF16).reshape(4, 32, 128)
    loads["proj"].wait()
    b.prs[:, :, :SW] = dot(b.pk[...].reshape(128, TW), b.projv[...], NN).astype(BF16).reshape(4, 32, SW)
    t3 = [send(b.prs.at[(t + o) % 4], b.t3r.at[o - 1], on_tp(o)) for o in range(1, 4)]

    gather_forward(hidden)
    for c in t3:
        c.wait_recv()
    acc = b.prs[t].astype(F32)
    for o in range(3):
        acc = acc + b.t3r[o].astype(F32)
    squares = acc[:, SW : SW + 1] + acc[:, SW + 128 : SW + 129]
    b.t4s[...] = acc[:, :SW] * lax.rsqrt(squares / TEACHER_WIDTH + EPS)
    t4 = describe(b.t4s, b.t4r, swapped)

    @pl.when(s != f)
    def _():
        t4.start()

    @pl.when(s == f)
    def _():
        b.t4r[...] = b.t4s[...]

    loads["wd"].wait()
    gather_end(hidden)

    factors = gather_start(b.aa)
    for k in range(8):
        r = dot(b.ht[k // 2, k % 2], b.wd[...], TN)
        b.pb[k] = r.astype(BF16).reshape(4, 2, 16, SW)
    d1 = send(b.pb.at[:, :, 1 - core], b.d1r, other_core)
    stores.append(pltpu.make_async_copy(b.ht, outs[1], out_sem.at[1]))
    stores[1].start()
    d1.wait_recv()
    for k in range(8):
        b.q[k] = (b.pb[k, :, core].astype(F32) + b.d1r[k].astype(F32)).astype(BF16)
    d2 = [send(b.q.at[:, (x + o) % 4], b.d2r.at[o - 1], on_x(o)) for o in (2, 1, 3)]
    for c in d2:
        c.wait_recv()
    for k in range(8):
        acc = b.q[k, x].astype(F32)
        for o in range(3):
            acc = acc + b.d2r[o, k].astype(F32)
        b.r[k // 2, k % 2] = acc.astype(BF16)
    d3 = [send(b.r.at[(t + o) % 4], b.d3r.at[o - 1], on_tp(o)) for o in range(1, 4)]
    gather_forward(factors)

    @pl.when(s != f)
    def _():
        t4.wait_recv()

    for e in range(2):

        @pl.when(f != 2 * t + e)
        def _():
            describe(b.xr.at[e], b.xr.at[e], {"fsdp": (f + 1) % 8}, e).wait_recv()

    for c in d3:
        c.wait_recv()
    for e in range(2):
        acc = b.r[t, e].astype(F32)
        for o in range(3):
            acc = acc + b.d3r[o, e].astype(F32)
        error = b.xr[e].astype(F32) + acc - b.t4r[e * 16 : (e + 1) * 16]
        b.dl[2 * t + e, s] = (error / ROWS).astype(BF16)

    own = b.dl.at[pl.ds(2 * t, 2), s]
    for c in [send(own, own, on_tp(o)) for o in range(1, 4)]:
        c.wait_recv()
    e2 = spread_start(lambda k: b.dl.at[:, k])
    spread_forward(e2)
    gather_end(factors)
    stores.append(pltpu.make_async_copy(b.aa, outs[3], out_sem.at[3]))
    stores[2].start()
    spread_end(e2)

    def d_hidden(z):
        four = jnp.concatenate([b.dl[2 * k + z].reshape(128, SW) for k in range(4)], axis=0)
        return dot(b.wd[...], four, NT)

    copies = reduce_start(b.h1, b.hr, d_hidden)
    stores.append(pltpu.make_async_copy(b.dl, outs[2], out_sem.at[2]))
    stores[3].start()
    across = reduce_across(copies, b.h1, b.hr, b.hzs, b.hzr, HW)
    for c in copies[1]:
        c.wait_recv()
    across.wait_recv()
    for k in range(0, HW, CHUNK):
        cut = slice(k, k + CHUNK)
        b.dh[y, zh, cut] = (partial_sum(b.h1, b.hr, 1, cut) + b.hzr[cut].astype(F32)).astype(BF16)
    last = gather_start(b.dh)
    gather_forward(last)
    gather_end(last)
    stores.append(pltpu.make_async_copy(b.dh, outs[4], out_sem.at[4]))
    stores[4].start()

    for c in started:
        c.wait_send()

    @pl.when(s != f)
    def _():
        t4.wait_send()

    @pl.when(y == t)
    def _():
        for c in xsends:
            c.wait_send()

    for c in stores:
        c.wait()


def gradients(nt, ht, dl, aa, dh, gate_o, up_o, down_o, d_gate, d_up, hidden):
    @pl.when(pl.program_id(0) == 0)
    def _():
        for k in range(8):
            here = slice(128 * k, 128 * (k + 1))
            d = dh[k].astype(F32)
            d_gate[:, here] = (d * aa[k, :HW].astype(F32)).astype(BF16)
            d_up[:, here] = (d * aa[k, HW:].astype(F32)).astype(BF16)
            hidden[:, here] = ht[k]

    normed = jnp.concatenate([nt[k] for k in range(8)], axis=1)
    gate_o[...] = dot(d_gate[...], normed, NT)
    up_o[...] = dot(d_up[...], normed, NT)
    down_o[...] = dot(hidden[...], dl[...], NN)


def on_device(
    teacher_updates, layer_map, route, projector, student_in, norm_gain, w_gate, w_up, w_down
):
    vmem = pl.BlockSpec(memory_space=pltpu.VMEM)
    hbm = pl.BlockSpec(memory_space=pl.ANY)
    shapes = {name: (shape, kind) for name, shape, kind in SCRATCH}
    nt, ht, dl, aa, dh = pl.pallas_call(
        kernel,
        out_shape=[jax.ShapeDtypeStruct(*shapes[name]) for name in OUTS],
        in_specs=[hbm, vmem, vmem, hbm, vmem, vmem, hbm, hbm, hbm],
        out_specs=[hbm] * len(OUTS),
        scratch_shapes=[pltpu.VMEM(shape, kind) for _, shape, kind in SCRATCH]
        + [pltpu.SemaphoreType.DMA((n,)) for n in (N_SEM, N_SEM, 5, len(OUTS))],
        compiler_params=pltpu.CompilerParams(
            collective_id=0, has_side_effects=True, vmem_limit_bytes=56 * 1024 * 1024
        ),
    )(
        teacher_updates.reshape(32, 4, TW),
        layer_map,
        route,
        projector,
        student_in.reshape(8, 16, STUDENT_WIDTH),
        norm_gain.reshape(1, STUDENT_WIDTH),
        w_gate.T,
        w_up.T,
        w_down,
    )

    def whole(shape):
        return pl.BlockSpec(shape, lambda i: (0,) * len(shape))

    gate_grad, up_grad, down_grad = pl.pallas_call(
        gradients,
        grid=(SW // 128,),
        out_shape=[jax.ShapeDtypeStruct((HW, SW), F32)] * 3,
        in_specs=[
            pl.BlockSpec((8, 128, 128), lambda i: (0, i, 0)),
            whole((8, HW, 128)),
            pl.BlockSpec((1024, 128), lambda i: (0, i)),
            whole((8, 2 * HW, 128)),
            whole((8, HW, 128)),
        ],
        out_specs=[pl.BlockSpec((HW, 128), lambda i: (0, i))] * 3,
        scratch_shapes=[pltpu.VMEM((HW, 1024), BF16)] * 3,
        compiler_params=pltpu.CompilerParams(vmem_limit_bytes=56 * 1024 * 1024),
    )(
        nt.reshape(8, SW, 128),
        ht.reshape(8, HW, 128),
        dl.reshape(1024, SW),
        aa.reshape(8, 2 * HW, 128),
        dh.reshape(8, HW, 128),
    )
    return gate_grad.T, up_grad.T, down_grad


def solution(mesh):
    placed = (
        P("section", "fsdp", None, "tp"),
        P(),
        P(),
        P("tp", "section"),
        P("fsdp", None, None, None),
        P(),
        P("fsdp", ("section", "tp")),
        P("fsdp", ("section", "tp")),
        P(("section", "tp"), "fsdp"),
    )
    return jax.shard_map(
        on_device,
        mesh=mesh,
        in_specs=placed,
        out_specs=(
            P("fsdp", ("section", "tp")),
            P("fsdp", ("section", "tp")),
            P(("section", "tp"), "fsdp"),
        ),
        check_vma=False,
    )
```

```python
import jax
import jax.numpy as jnp
from jax import lax
from jax.experimental import pallas as pl
from jax.experimental.pallas import tpu as pltpu
from jax.sharding import PartitionSpec as P

MESH = pl.DeviceIdType.MESH
EPS = 1e-05
F32 = jnp.float32
BF16 = jnp.bfloat16

TW = 4096
SW = 640
SUB = 80
HW = 400
TEACHER_WIDTH = 16384
STUDENT_WIDTH = 5120
ROWS = 4

NN = (((1,), (0,)), ((), ()))
NT = (((1,), (1,)), ((), ()))
TN = (((0,), (0,)), ((), ()))


def dot(a, b, dims):
    return lax.dot_general(a, b, dims, preferred_element_type=F32)


SCRATCH = (
    ("updv", (32, 4, TW), BF16),
    ("projv", (TW, SW), BF16),
    ("wg", (HW, SW), BF16),
    ("wu", (HW, SW), BF16),
    ("wd", (HW, SW), BF16),
    ("u", (8, 16, TW), BF16),
    ("t1r", (8, 16, TW), BF16),
    ("pk", (8, 16, TW), BF16),
    ("prs", (4, 32, SW + 256), BF16),
    ("t3r", (3, 32, SW + 256), BF16),
    ("t4s", (32, SW), BF16),
    ("t4r", (32, SW), BF16),
    ("xr", (2, 16, SW), BF16),
    ("a1s", (8, SUB, 128), BF16),
    ("nt", (4, 2, 8, SUB, 128), BF16),
    ("g1", (2, 4, 2 * HW, 128), BF16),
    ("gr", (2, 3, 2 * HW, 128), BF16),
    ("gzs", (2 * HW, 128), BF16),
    ("gzr", (2 * HW, 128), BF16),
    ("aa", (4, 2, 2 * HW, 128), BF16),
    ("ht", (4, 2, HW, 128), BF16),
    ("pb0", (8, 4, 2, 16, 384), BF16),
    ("d1r0", (8, 4, 16, 384), BF16),
    ("q0", (8, 4, 16, 384), BF16),
    ("d2r0", (3, 8, 16, 384), BF16),
    ("r0", (4, 2, 16, 384), BF16),
    ("d3r0", (3, 2, 16, 384), BF16),
    ("dl0", (8, 8, 16, 384), BF16),
    ("pb1", (8, 4, 2, 16, 256), BF16),
    ("d1r1", (8, 4, 16, 256), BF16),
    ("q1", (8, 4, 16, 256), BF16),
    ("d2r1", (3, 8, 16, 256), BF16),
    ("r1", (4, 2, 16, 256), BF16),
    ("d3r1", (3, 2, 16, 256), BF16),
    ("dl1", (8, 8, 16, 256), BF16),
    ("hacc", (2, HW, 512), F32),
    ("down", (HW, SW), F32),
    ("h1", (2, 4, HW, 128), BF16),
    ("hr", (2, 3, HW, 128), BF16),
    ("hzs", (HW, 128), BF16),
    ("hzr", (HW, 128), BF16),
    ("dh", (4, 2, HW, 128), BF16),
)
N_SEM = 192
OUTS = (
    ((4, 2, 8, SUB, 128), BF16),
    ((HW, SW), F32),
    ((4, 2, 2 * HW, 128), BF16),
    ((4, 2, HW, 128), BF16),
)
HALF = 208
HIDDEN = ((0, HALF), (HALF, HW))
BOTH = ((0, 2 * HALF), (2 * HALF, 2 * HW))
COLUMNS = ((0, 384), (384, SW))


class Refs:
    pass


def selection(layer_map, route, f, s):
    lane = lax.broadcasted_iota(jnp.int32, (32, 128), 1)
    slot = lax.broadcasted_iota(jnp.int32, (32, 128), 0)
    widen = jnp.where(lane // ROWS == slot, 1.0, 0.0).astype(BF16)
    mine = lax.broadcasted_iota(jnp.int32, (8, 128), 0) == f

    def row(table):
        wide = dot(table[...].astype(F32).astype(BF16), widen, NN)
        return jnp.sum(jnp.where(mine, wide, 0.0), axis=0, keepdims=True)

    dest, layer = row(route), row(layer_map)
    across = jnp.broadcast_to(dest, (128, 128))
    a = lax.broadcasted_iota(jnp.int32, (128, 128), 0)
    c = lax.broadcasted_iota(jnp.int32, (128, 128), 1)
    earlier = (across.T == across) & (a // ROWS < c // ROWS) & (a % ROWS == 0)
    rank = jnp.sum(jnp.where(earlier, 1.0, 0.0), axis=0, keepdims=True)
    place = (dest * 4.0 + rank) * ROWS + (c[0:1] % ROWS).astype(F32)
    place = jnp.where(layer >= s.astype(F32), place, -1.0)
    return jnp.where(a.astype(F32) == place, 1.0, 0.0).astype(BF16)


def kernel(upd, layer_map, route, proj, xin, gain, wg, wu, wd, *rest):
    outs, scratch = rest[: len(OUTS)], rest[len(OUTS) :]
    b = Refs()
    for (name, _, _), ref in zip(SCRATCH, scratch):
        setattr(b, name, ref)
    send_sem, recv_sem, in_sem, out_sem = scratch[len(SCRATCH) :]
    s = lax.axis_index("section")
    t = lax.axis_index("tp")
    f = lax.axis_index("fsdp")
    x, core = s // 2, s % 2
    y, zh = f // 2, f % 2
    far_z = 1 - zh
    used = [2]
    started = []

    def describe(src, dst, dev, sem=None):
        if sem is None:
            sem = used[0]
            used[0] += 1
        return pltpu.make_async_remote_copy(
            src_ref=src,
            dst_ref=dst,
            send_sem=send_sem.at[sem],
            recv_sem=recv_sem.at[sem],
            device_id=dev,
            device_id_type=MESH,
        )

    def send(src, dst, dev):
        copy = describe(src, dst, dev)
        copy.start()
        started.append(copy)
        return copy

    def on_x(o):
        return {"section": (x + o) % 4 * 2 + core}

    def on_y(o):
        return {"fsdp": (y + o) % 4 * 2 + zh}

    def on_tp(o):
        return {"tp": (t + o) % 4}

    other_core = {"section": x * 2 + 1 - core}
    other_z = {"fsdp": y * 2 + far_z}
    swapped = {"section": f, "fsdp": s}

    barrier = pltpu.get_barrier_semaphore()
    for o in range(1, 8):
        pl.semaphore_signal(barrier, inc=1, device_id={"section": (s + o) % 8}, device_id_type=MESH)
        pl.semaphore_signal(barrier, inc=1, device_id={"fsdp": (f + o) % 8}, device_id_type=MESH)
    for o in range(1, 4):
        pl.semaphore_signal(barrier, inc=1, device_id=on_tp(o), device_id_type=MESH)

    @pl.when(s != f)
    def _():
        pl.semaphore_signal(barrier, inc=1, device_id=swapped, device_id_type=MESH)

    loads = {}
    for k, (name, src, dst) in enumerate(
        (("wg", wg, b.wg), ("wu", wu, b.wu), ("upd", upd, b.updv), ("proj", proj, b.projv), ("wd", wd, b.wd))
    ):
        loads[name] = pltpu.make_async_copy(src, dst, in_sem.at[k])
        loads[name].start()

    def student(k):
        return xin[:, :, k * SW : (k + 1) * SW].reshape(128, SW).astype(F32)

    total = jnp.zeros((128, 128), F32)
    for k in range(8):
        v = student(k)
        for c in range(0, SW, 128):
            total = total + v[:, c : c + 128] * v[:, c : c + 128]
    total = jnp.sum(total, axis=1, keepdims=True)
    inv = lax.rsqrt(total / STUDENT_WIDTH + EPS)
    rows = lax.broadcasted_iota(jnp.int32, (SUB, SW), 0)
    cols = lax.broadcasted_iota(jnp.int32, (SUB, SW), 1)
    sel = jnp.where(cols == rows + s * SUB, 1.0, 0.0).astype(BF16)
    for k in range(8):
        normed = (student(k) * inv * gain[:, k * SW : (k + 1) * SW]).astype(BF16)
        b.a1s[k] = dot(sel, normed, NT).astype(BF16)

    pl.semaphore_wait(barrier, jnp.where(s == f, 17, 18))

    a1 = {}
    for dz, dy in ((1, 0), (1, 1), (1, 3), (1, 2), (0, 1), (0, 3), (0, 2)):
        k = (y + dy) % 4 * 2 + (zh + dz) % 2
        a1[dz, dy] = send(b.a1s.at[k], b.nt.at[y, zh, s], {"fsdp": k})
    b.nt[y, zh, s] = b.a1s[f]

    xsends = []
    for o in range(1, 8):
        k = (f + o) % 8
        c = pltpu.make_async_remote_copy(
            src_ref=xin.at[s, :, pl.ds(pl.multiple_of(k * SW, 128), SW)],
            dst_ref=b.xr.at[zh],
            send_sem=send_sem.at[used[0]],
            recv_sem=recv_sem.at[zh],
            device_id={"fsdp": k},
            device_id_type=MESH,
        )
        used[0] += 1
        xsends.append(c)

    @pl.when(y == t)
    def _():
        for c in xsends:
            c.start()
        b.xr[zh] = xin[s, :, pl.ds(pl.multiple_of(f * SW, 128), SW)]

    def spread_start(at):
        copies = [send(at(s), at(s), on_x(o)) for o in range(1, 4)]
        across = [send(at(s), at(s), other_core)]
        return at, copies, across

    def spread_forward(state):
        at, copies, across = state
        for o in range(1, 4):
            copies[o - 1].wait_recv()
            k = (x - o + 4) % 4 * 2 + core
            across.append(send(at(k), at(k), other_core))

    def spread_end(state):
        for c in state[2]:
            c.wait_recv()

    for dy in (1, 2, 3):
        a1[0, dy].wait_recv()
    near = spread_start(lambda k: b.nt.at[:, zh, k])

    perm = selection(layer_map, route, f, s)
    loads["upd"].wait()
    for k in range(4):
        cut = slice(k * (TW // 4), (k + 1) * (TW // 4))
        part = b.updv[:, :, cut].reshape(128, TW // 4)
        b.u[:, :, cut] = dot(perm, part, NN).astype(BF16).reshape(8, 16, TW // 4)

    for dy in (0, 1, 2, 3):
        a1[1, dy].wait_recv()
    far = spread_start(lambda k: b.nt.at[:, far_z, k])
    loads["wg"].wait()
    loads["wu"].wait()

    def rows_of(chunk):
        return pl.ds(chunk[0], chunk[1] - chunk[0])

    def reduce_send(src, got, h, chunk):
        part = rows_of(chunk)
        return [send(src.at[h, (y + o) % 4, part], got.at[h, o - 1, part], on_y(o)) for o in (2, 1, 3)]

    def partial_sum(src, got, h, low, high):
        acc = src[h, y, low:high].astype(F32)
        for o in range(3):
            acc = acc + got[h, o, low:high].astype(F32)
        return acc

    def reduce_across(copies, src, got, zs, zr, chunk):
        for c in copies:
            c.wait_recv()
        for k in range(chunk[0], chunk[1], 16 * 13):
            top = min(k + 16 * 13, chunk[1])
            zs[k:top] = partial_sum(src, got, 0, k, top).astype(BF16)
        return send(zs.at[rows_of(chunk)], zr.at[rows_of(chunk)], other_z)

    def gather_start(buf, chunk):
        own = buf.at[y, zh, rows_of(chunk)]
        far = send(own, own, other_z)
        return buf, chunk, far, [send(own, own, on_y(o)) for o in (2, 1, 3)]

    def gather_forward(state):
        buf, chunk, far, copies = state
        far.wait_recv()
        got = buf.at[y, far_z, rows_of(chunk)]
        copies += [send(got, got, on_y(o)) for o in (2, 1, 3)]

    def gather_end(state):
        for c in state[3]:
            c.wait_recv()

    def gate_up(h, z):
        four = jnp.concatenate([b.nt[k, z].reshape(SW, 128) for k in range(4)], axis=1)
        for w, put in ((b.wg, 0), (b.wu, 1)):
            r = dot(w[...], four, NN).astype(BF16)
            for k in range(4):
                lanes = slice(128 * k, 128 * (k + 1))
                b.g1[h, k, put * HALF : (put + 1) * HALF] = r[:HALF, lanes]
                low = 2 * HALF + put * (HW - HALF)
                b.g1[h, k, low : low + HW - HALF] = r[HALF:, lanes]

    spread_forward(near)
    spread_end(near)
    gate_up(1, zh)
    near_rows = [reduce_send(b.g1, b.gr, 1, BOTH[0])]
    spread_forward(far)
    t1 = []
    for o in range(1, 8):
        k = (s + o) % 8
        t1.append(send(b.u.at[k], b.t1r.at[s], {"section": k}))
    spread_end(far)
    gate_up(0, far_z)
    far_rows = [reduce_send(b.g1, b.gr, 0, chunk) for chunk in BOTH]
    near_rows.append(reduce_send(b.g1, b.gr, 1, BOTH[1]))
    stores = [pltpu.make_async_copy(b.nt, outs[0], out_sem.at[0])]
    stores[0].start()
    across = [reduce_across(far_rows[0], b.g1, b.gr, b.gzs, b.gzr, BOTH[0])]

    for c in t1:
        c.wait_recv()
    for k in range(4):
        cut = slice(k * (TW // 4), (k + 1) * (TW // 4))
        acc = b.u[s, :, cut].astype(F32)
        for o in range(1, 8):
            acc = acc + b.t1r[(s + o) % 8, :, cut].astype(F32)
        b.pk[s, :, cut] = acc.astype(BF16)
    t2 = spread_start(lambda k: b.pk.at[k])
    across.append(reduce_across(far_rows[1], b.g1, b.gr, b.gzs, b.gzr, BOTH[1]))

    hidden = []
    for n in range(2):
        for c in near_rows[n]:
            c.wait_recv()
        across[n].wait_recv()
        low, mid, high = BOTH[n][0], (BOTH[n][0] + BOTH[n][1]) // 2, BOTH[n][1]
        gate = partial_sum(b.g1, b.gr, 1, low, mid) + b.gzr[low:mid].astype(F32)
        up = partial_sum(b.g1, b.gr, 1, mid, high) + b.gzr[mid:high].astype(F32)
        sig = 1.0 / (1.0 + jnp.exp(-gate))
        b.ht[y, zh, HIDDEN[n][0] : HIDDEN[n][1]] = (gate * sig * up).astype(BF16)
        hidden.append(gather_start(b.ht, HIDDEN[n]))
        b.aa[y, zh, low:mid] = (up * sig * (1.0 + gate * (1.0 - sig))).astype(BF16)
        b.aa[y, zh, mid:high] = (gate * sig).astype(BF16)
    gather_forward(hidden[0])
    spread_forward(t2)
    gather_forward(hidden[1])

    spread_end(t2)
    squares = jnp.zeros((128, 1), F32)
    for k in range(4):
        v = b.pk[:, :, k * (TW // 4) : (k + 1) * (TW // 4)].reshape(128, TW // 4).astype(F32)
        squares = squares + jnp.sum(v * v, axis=1, keepdims=True)
    squares = jnp.broadcast_to(squares, (128, 128))
    high = squares.astype(BF16)
    b.prs[:, :, SW : SW + 128] = high.reshape(4, 32, 128)
    b.prs[:, :, SW + 128 :] = (squares - high.astype(F32)).astype(BF16).reshape(4, 32, 128)
    loads["proj"].wait()
    b.prs[:, :, :SW] = dot(b.pk[...].reshape(128, TW), b.projv[...], NN).astype(BF16).reshape(4, 32, SW)
    t3 = [send(b.prs.at[(t + o) % 4], b.t3r.at[o - 1], on_tp(o)) for o in range(1, 4)]
    loads["wd"].wait()
    for n in range(2):
        gather_end(hidden[n])

    pb, d1r, q = (b.pb0, b.pb1), (b.d1r0, b.d1r1), (b.q0, b.q1)
    d2r, r, d3r, dl = (b.d2r0, b.d2r1), (b.r0, b.r1), (b.d3r0, b.d3r1), (b.dl0, b.dl1)
    for k in range(8):
        m = dot(b.ht[k // 2, k % 2], b.wd[...], TN).astype(BF16)
        for n, (low, high) in enumerate(COLUMNS):
            pb[n][k] = m[:, low:high].reshape(4, 2, 16, high - low)
    d1 = [send(pb[n].at[:, :, 1 - core], d1r[n], other_core) for n in range(2)]
    factors = gather_start(b.aa, (0, 2 * HW))
    d2 = []
    for n in range(2):
        d1[n].wait_recv()
        for k in range(8):
            q[n][k] = (pb[n][k, :, core].astype(F32) + d1r[n][k].astype(F32)).astype(BF16)
        d2.append([send(q[n].at[:, (x + o) % 4], d2r[n].at[o - 1], on_x(o)) for o in (2, 1, 3)])

    for c in t3:
        c.wait_recv()
    acc = b.prs[t].astype(F32)
    for o in range(3):
        acc = acc + b.t3r[o].astype(F32)
    squares = acc[:, SW : SW + 1] + acc[:, SW + 128 : SW + 129]
    b.t4s[...] = (acc[:, :SW] * lax.rsqrt(squares / TEACHER_WIDTH + EPS)).astype(BF16)
    t4 = describe(b.t4s, b.t4r, swapped)

    @pl.when(s != f)
    def _():
        t4.start()

    @pl.when(s == f)
    def _():
        b.t4r[...] = b.t4s[...]

    d3 = []
    for n in range(2):
        for c in d2[n]:
            c.wait_recv()
        for k in range(8):
            acc = q[n][k, x].astype(F32)
            for o in range(3):
                acc = acc + d2r[n][o, k].astype(F32)
            r[n][k // 2, k % 2] = acc.astype(BF16)
        d3.append([send(r[n].at[(t + o) % 4], d3r[n].at[o - 1], on_tp(o)) for o in range(1, 4)])
    gather_forward(factors)

    @pl.when(s != f)
    def _():
        t4.wait_recv()

    for e in range(2):

        @pl.when(f != 2 * t + e)
        def _():
            describe(b.xr.at[e], b.xr.at[e], {"fsdp": (f + 1) % 8}, e).wait_recv()

    e1 = []
    for n, (low, high) in enumerate(COLUMNS):
        for c in d3[n]:
            c.wait_recv()
        for e in range(2):
            acc = r[n][t, e].astype(F32)
            for o in range(3):
                acc = acc + d3r[n][o, e].astype(F32)
            error = b.xr[e, :, low:high].astype(F32) + acc - b.t4r[e * 16 : (e + 1) * 16, low:high].astype(F32)
            dl[n][2 * t + e, s] = (error / ROWS).astype(BF16)
        own = dl[n].at[pl.ds(2 * t, 2), s]
        e1.append([send(own, own, on_tp(o)) for o in range(1, 4)])
    e2 = []
    for n in range(2):
        for c in e1[n]:
            c.wait_recv()
        e2.append(spread_start(lambda k, buf=dl[n]: buf.at[:, k]))

    def d_hidden(n, z):
        low, high = COLUMNS[n]
        four = jnp.concatenate([dl[n][2 * k + z].reshape(128, high - low) for k in range(4)], axis=0)
        return dot(b.wd[:, low:high], four, NT)

    spread_forward(e2[0])
    spread_end(e2[0])
    b.hacc[0] = d_hidden(0, far_z)
    b.hacc[1] = d_hidden(0, zh)
    spread_forward(e2[1])
    spread_end(e2[1])
    copies = []
    for h, z in ((0, far_z), (1, zh)):
        m = (b.hacc[h] + d_hidden(1, z)).astype(BF16)
        for k in range(4):
            b.h1[h, k] = m[:, 128 * k : 128 * (k + 1)]
        copies.append([reduce_send(b.h1, b.hr, h, chunk) for chunk in HIDDEN])
    gather_end(factors)
    stores.append(pltpu.make_async_copy(b.aa, outs[2], out_sem.at[2]))
    stores[-1].start()
    across = [reduce_across(copies[0][n], b.h1, b.hr, b.hzs, b.hzr, HIDDEN[n]) for n in range(2)]

    units = jnp.concatenate([b.ht[k // 2, k % 2] for k in range(8)], axis=1)
    for n, (low, high) in enumerate(COLUMNS):
        b.down[:, low:high] = dot(units, dl[n][...].reshape(1024, high - low), NN)
    stores.append(pltpu.make_async_copy(b.down, outs[1], out_sem.at[1]))
    stores[-1].start()
    last = []
    for n, (low, high) in enumerate(HIDDEN):
        for c in copies[1][n]:
            c.wait_recv()
        across[n].wait_recv()
        b.dh[y, zh, low:high] = (partial_sum(b.h1, b.hr, 1, low, high) + b.hzr[low:high].astype(F32)).astype(BF16)
        last.append(gather_start(b.dh, HIDDEN[n]))
    for n in range(2):
        gather_forward(last[n])
    for n in range(2):
        gather_end(last[n])
        part = rows_of(HIDDEN[n])
        stores.append(pltpu.make_async_copy(b.dh.at[:, :, part], outs[3].at[:, :, part], out_sem.at[3 + n]))
        stores[-1].start()

    for c in started:
        c.wait_send()

    @pl.when(s != f)
    def _():
        t4.wait_send()

    @pl.when(y == t)
    def _():
        for c in xsends:
            c.wait_send()

    for c in stores:
        c.wait()
    assert used[0] <= N_SEM


def gradients(nt, down, aa, dh, gate_o, up_o, down_o, nt_v, aa_v, dh_v, grad_v, down_v, sems):
    loads = [
        pltpu.make_async_copy(src, dst, sems.at[k])
        for k, (src, dst) in enumerate(((dh, dh_v), (aa, aa_v), (nt, nt_v), (down, down_v)))
    ]
    for c in loads:
        c.start()
    loads[0].wait()
    loads[1].wait()

    def hidden_grad(put):
        parts = []
        for n in range(2):
            (low, high), (first, last) = HIDDEN[n], BOTH[n]
            rows = slice(first + put * (high - low), first + (put + 1) * (high - low))
            parts.append(
                jnp.concatenate(
                    [(dh_v[k, low:high].astype(F32) * aa_v[k, rows].astype(F32)).astype(BF16) for k in range(8)],
                    axis=1,
                )
            )
        return jnp.concatenate(parts, axis=0)

    d_gate, d_up = hidden_grad(0), hidden_grad(1)
    loads[3].wait()
    down_store = pltpu.make_async_copy(down_v, down_o, sems.at[6])
    down_store.start()
    loads[2].wait()
    normed = jnp.concatenate([nt_v[k] for k in range(8)], axis=1)
    grad_v[0] = dot(d_gate, normed, NT)
    gate_store = pltpu.make_async_copy(grad_v.at[0], gate_o, sems.at[4])
    gate_store.start()
    grad_v[1] = dot(d_up, normed, NT)
    up_store = pltpu.make_async_copy(grad_v.at[1], up_o, sems.at[5])
    up_store.start()
    down_store.wait()
    gate_store.wait()
    up_store.wait()


def on_device(
    teacher_updates, layer_map, route, projector, student_in, norm_gain, w_gate, w_up, w_down
):
    vmem = pl.BlockSpec(memory_space=pltpu.VMEM)
    hbm = pl.BlockSpec(memory_space=pl.ANY)
    nt, down, aa, dh = pl.pallas_call(
        kernel,
        out_shape=[jax.ShapeDtypeStruct(*out) for out in OUTS],
        in_specs=[hbm, vmem, vmem, hbm, vmem, vmem, hbm, hbm, hbm],
        out_specs=[hbm] * len(OUTS),
        scratch_shapes=[pltpu.VMEM(shape, kind) for _, shape, kind in SCRATCH]
        + [pltpu.SemaphoreType.DMA((n,)) for n in (N_SEM, N_SEM, 5, 5)],
        compiler_params=pltpu.CompilerParams(
            collective_id=0, has_side_effects=True, vmem_limit_bytes=56 * 1024 * 1024
        ),
    )(
        teacher_updates.reshape(32, 4, TW),
        layer_map,
        route,
        projector,
        student_in.reshape(8, 16, STUDENT_WIDTH),
        norm_gain.reshape(1, STUDENT_WIDTH),
        w_gate.T,
        w_up.T,
        w_down,
    )

    gate_grad, up_grad, down_grad = pl.pallas_call(
        gradients,
        out_shape=[jax.ShapeDtypeStruct((HW, SW), F32)] * 3,
        in_specs=[hbm] * 4,
        out_specs=[hbm] * 3,
        scratch_shapes=[
            pltpu.VMEM((8, SW, 128), BF16),
            pltpu.VMEM((8, 2 * HW, 128), BF16),
            pltpu.VMEM((8, HW, 128), BF16),
            pltpu.VMEM((2, HW, SW), F32),
            pltpu.VMEM((HW, SW), F32),
            pltpu.SemaphoreType.DMA((7,)),
        ],
        compiler_params=pltpu.CompilerParams(vmem_limit_bytes=56 * 1024 * 1024),
    )(nt.reshape(8, SW, 128), down, aa.reshape(8, 2 * HW, 128), dh.reshape(8, HW, 128))
    return gate_grad.T, up_grad.T, down_grad


def solution(mesh):
    placed = (
        P("section", "fsdp", None, "tp"),
        P(),
        P(),
        P("tp", "section"),
        P("fsdp", None, None, None),
        P(),
        P("fsdp", ("section", "tp")),
        P("fsdp", ("section", "tp")),
        P(("section", "tp"), "fsdp"),
    )
    return jax.shard_map(
        on_device,
        mesh=mesh,
        in_specs=placed,
        out_specs=(
            P("fsdp", ("section", "tp")),
            P("fsdp", ("section", "tp")),
            P(("section", "tp"), "fsdp"),
        ),
        check_vma=False,
    )
```

```python
import jax
import jax.numpy as jnp
from jax import lax
from jax.experimental import pallas as pl
from jax.experimental.pallas import tpu as pltpu
from jax.sharding import PartitionSpec as P

MESH = pl.DeviceIdType.MESH
EPS = 1e-05
F32 = jnp.float32
BF16 = jnp.bfloat16

TW = 4096
SW = 640
SUB = 80
HW = 400
TEACHER_WIDTH = 16384
STUDENT_WIDTH = 5120
ROWS = 4

NN = (((1,), (0,)), ((), ()))
NT = (((1,), (1,)), ((), ()))
TN = (((0,), (0,)), ((), ()))


def dot(a, b, dims):
    return lax.dot_general(a, b, dims, preferred_element_type=F32)


SCRATCH = (
    ("updv", (32, 4, TW), BF16),
    ("projv", (TW, SW), BF16),
    ("wg", (HW, SW), BF16),
    ("wu", (HW, SW), BF16),
    ("wd", (HW, SW), BF16),
    ("u", (8, 16, TW), BF16),
    ("t1r", (8, 16, TW), BF16),
    ("pk", (8, 16, TW), BF16),
    ("prs", (4, 32, SW + 256), BF16),
    ("t3r", (3, 32, SW + 256), BF16),
    ("t4s", (32, SW), BF16),
    ("t4r", (32, SW), BF16),
    ("xr", (2, 16, SW), BF16),
    ("a1s", (7, SUB, 128), BF16),
    ("nt", (4, 2, 8, SUB, 128), BF16),
    ("g1", (2, 4, 2 * HW, 128), BF16),
    ("gr", (2, 3, 2 * HW, 128), BF16),
    ("gzs", (2 * HW, 128), BF16),
    ("gzr", (2 * HW, 128), BF16),
    ("aa", (4, 2, 2 * HW, 128), BF16),
    ("ht", (4, 2, HW, 128), BF16),
    ("pb0", (8, 4, 2, 16, 384), BF16),
    ("d1r0", (8, 4, 16, 384), BF16),
    ("q0", (8, 4, 16, 384), BF16),
    ("d2r0", (3, 8, 16, 384), BF16),
    ("r0", (4, 2, 16, 384), BF16),
    ("d3r0", (3, 2, 16, 384), BF16),
    ("dl0", (8, 8, 16, 384), BF16),
    ("pb1", (8, 4, 2, 16, 256), BF16),
    ("d1r1", (8, 4, 16, 256), BF16),
    ("q1", (8, 4, 16, 256), BF16),
    ("d2r1", (3, 8, 16, 256), BF16),
    ("r1", (4, 2, 16, 256), BF16),
    ("d3r1", (3, 2, 16, 256), BF16),
    ("dl1", (8, 8, 16, 256), BF16),
    ("hacc", (2, HW, 512), F32),
    ("down", (HW, SW), F32),
    ("h1", (2, 4, HW, 128), BF16),
    ("hr", (2, 3, HW, 128), BF16),
    ("hzs", (HW, 128), BF16),
    ("hzr", (HW, 128), BF16),
    ("dh", (4, 2, HW, 128), BF16),
)
N_SEM = 192
OUTS = (
    ((4, 2, 8, SUB, 128), BF16),
    ((HW, SW), F32),
    ((4, 2, 2 * HW, 128), BF16),
    ((4, 2, HW, 128), BF16),
)
HALF = 208
HIDDEN = ((0, HALF), (HALF, HW))
BOTH = ((0, 2 * HALF), (2 * HALF, 2 * HW))
COLUMNS = ((0, 384), (384, SW))


class Refs:
    pass


def selection(layer_map, route, f, s):
    lane = lax.broadcasted_iota(jnp.int32, (32, 128), 1)
    slot = lax.broadcasted_iota(jnp.int32, (32, 128), 0)
    widen = jnp.where(lane // ROWS == slot, 1.0, 0.0).astype(BF16)
    mine = lax.broadcasted_iota(jnp.int32, (8, 128), 0) == f

    def row(table):
        wide = dot(table[...].astype(F32).astype(BF16), widen, NN)
        return jnp.sum(jnp.where(mine, wide, 0.0), axis=0, keepdims=True)

    dest, layer = row(route), row(layer_map)
    across = jnp.broadcast_to(dest, (128, 128))
    a = lax.broadcasted_iota(jnp.int32, (128, 128), 0)
    c = lax.broadcasted_iota(jnp.int32, (128, 128), 1)
    earlier = (across.T == across) & (a // ROWS < c // ROWS) & (a % ROWS == 0)
    rank = jnp.sum(jnp.where(earlier, 1.0, 0.0), axis=0, keepdims=True)
    place = (dest * 4.0 + rank) * ROWS + (c[0:1] % ROWS).astype(F32)
    place = jnp.where(layer >= s.astype(F32), place, -1.0)
    return jnp.where(a.astype(F32) == place, 1.0, 0.0).astype(BF16)


def kernel(upd, layer_map, route, proj, xin, gain, wg, wu, wd, *rest):
    outs, scratch = rest[: len(OUTS)], rest[len(OUTS) :]
    b = Refs()
    for (name, _, _), ref in zip(SCRATCH, scratch):
        setattr(b, name, ref)
    send_sem, recv_sem, in_sem, out_sem = scratch[len(SCRATCH) :]
    s = lax.axis_index("section")
    t = lax.axis_index("tp")
    f = lax.axis_index("fsdp")
    x, core = s // 2, s % 2
    y, zh = f // 2, f % 2
    far_z = 1 - zh
    used = [2]
    started = []

    def describe(src, dst, dev, sem=None):
        if sem is None:
            sem = used[0]
            used[0] += 1
        return pltpu.make_async_remote_copy(
            src_ref=src,
            dst_ref=dst,
            send_sem=send_sem.at[sem],
            recv_sem=recv_sem.at[sem],
            device_id=dev,
            device_id_type=MESH,
        )

    def send(src, dst, dev):
        copy = describe(src, dst, dev)
        copy.start()
        started.append(copy)
        return copy

    def on_x(o):
        return {"section": (x + o) % 4 * 2 + core}

    def on_y(o):
        return {"fsdp": (y + o) % 4 * 2 + zh}

    def on_tp(o):
        return {"tp": (t + o) % 4}

    other_core = {"section": x * 2 + 1 - core}
    other_z = {"fsdp": y * 2 + far_z}
    swapped = {"section": f, "fsdp": s}

    barrier = pltpu.get_barrier_semaphore()
    for o in range(1, 8):
        pl.semaphore_signal(barrier, inc=1, device_id={"section": (s + o) % 8}, device_id_type=MESH)
        pl.semaphore_signal(barrier, inc=1, device_id={"fsdp": (f + o) % 8}, device_id_type=MESH)
    for o in range(1, 4):
        pl.semaphore_signal(barrier, inc=1, device_id=on_tp(o), device_id_type=MESH)

    @pl.when(s != f)
    def _():
        pl.semaphore_signal(barrier, inc=1, device_id=swapped, device_id_type=MESH)

    loads = {}
    for k, (name, src, dst) in enumerate(
        (("wg", wg, b.wg), ("wu", wu, b.wu), ("upd", upd, b.updv), ("proj", proj, b.projv), ("wd", wd, b.wd))
    ):
        loads[name] = pltpu.make_async_copy(src, dst, in_sem.at[k])
        loads[name].start()

    def student(k):
        return xin[:, :, k * SW : (k + 1) * SW].reshape(128, SW).astype(F32)

    total = jnp.zeros((128, 128), F32)
    for k in range(8):
        v = student(k)
        for c in range(0, SW, 128):
            total = total + v[:, c : c + 128] * v[:, c : c + 128]
    total = jnp.sum(total, axis=1, keepdims=True)
    inv = lax.rsqrt(total / STUDENT_WIDTH + EPS)
    rows = lax.broadcasted_iota(jnp.int32, (SUB, SW), 0)
    cols = lax.broadcasted_iota(jnp.int32, (SUB, SW), 1)
    sel = jnp.where(cols == rows + s * SUB, 1.0, 0.0).astype(BF16)
    pl.semaphore_wait(barrier, jnp.where(s == f, 17, 18))

    a1 = {}
    order = ((1, 0), (1, 1), (1, 3), (1, 2), (0, 1), (0, 3), (0, 2), (0, 0))
    for n, (dz, dy) in enumerate(order):
        k = (y + dy) % 4 * 2 + (zh + dz) % 2
        lanes = pl.ds(pl.multiple_of(k * SW, 128), SW)
        v = xin[:, :, lanes].reshape(128, SW).astype(F32)
        piece = dot(sel, (v * inv * gain[:, lanes]).astype(BF16), NT).astype(BF16)
        if n < 7:
            b.a1s[n] = piece
            a1[dz, dy] = send(b.a1s.at[n], b.nt.at[y, zh, s], {"fsdp": k})
        else:
            b.nt[y, zh, s] = piece

    xsends = []
    for o in range(1, 8):
        k = (f + o) % 8
        c = pltpu.make_async_remote_copy(
            src_ref=xin.at[s, :, pl.ds(pl.multiple_of(k * SW, 128), SW)],
            dst_ref=b.xr.at[zh],
            send_sem=send_sem.at[used[0]],
            recv_sem=recv_sem.at[zh],
            device_id={"fsdp": k},
            device_id_type=MESH,
        )
        used[0] += 1
        xsends.append(c)

    @pl.when(y == t)
    def _():
        for c in xsends:
            c.start()
        b.xr[zh] = xin[s, :, pl.ds(pl.multiple_of(f * SW, 128), SW)]

    def spread_start(at):
        copies = [send(at(s), at(s), on_x(o)) for o in range(1, 4)]
        across = [send(at(s), at(s), other_core)]
        return at, copies, across

    def spread_forward(state):
        at, copies, across = state
        for o in range(1, 4):
            copies[o - 1].wait_recv()
            k = (x - o + 4) % 4 * 2 + core
            across.append(send(at(k), at(k), other_core))

    def spread_end(state):
        for c in state[2]:
            c.wait_recv()

    for dy in (1, 2, 3):
        a1[0, dy].wait_recv()
    near = spread_start(lambda k: b.nt.at[:, zh, k])

    perm = selection(layer_map, route, f, s)
    loads["upd"].wait()
    for k in range(4):
        cut = slice(k * (TW // 4), (k + 1) * (TW // 4))
        part = b.updv[:, :, cut].reshape(128, TW // 4)
        b.u[:, :, cut] = dot(perm, part, NN).astype(BF16).reshape(8, 16, TW // 4)

    for dy in (0, 1, 2, 3):
        a1[1, dy].wait_recv()
    far = spread_start(lambda k: b.nt.at[:, far_z, k])
    loads["wg"].wait()
    loads["wu"].wait()

    def rows_of(chunk):
        return pl.ds(chunk[0], chunk[1] - chunk[0])

    def reduce_send(src, got, h, chunk):
        part = rows_of(chunk)
        return [send(src.at[h, (y + o) % 4, part], got.at[h, o - 1, part], on_y(o)) for o in (2, 1, 3)]

    def partial_sum(src, got, h, low, high):
        acc = src[h, y, low:high].astype(F32)
        for o in range(3):
            acc = acc + got[h, o, low:high].astype(F32)
        return acc

    def reduce_across(copies, src, got, zs, zr, chunk):
        for c in copies:
            c.wait_recv()
        for k in range(chunk[0], chunk[1], 16 * 13):
            top = min(k + 16 * 13, chunk[1])
            zs[k:top] = partial_sum(src, got, 0, k, top).astype(BF16)
        return send(zs.at[rows_of(chunk)], zr.at[rows_of(chunk)], other_z)

    def gather_start(buf, chunk):
        own = buf.at[y, zh, rows_of(chunk)]
        far = send(own, own, other_z)
        return buf, chunk, far, [send(own, own, on_y(o)) for o in (2, 1, 3)]

    def gather_forward(state):
        buf, chunk, far, copies = state
        far.wait_recv()
        got = buf.at[y, far_z, rows_of(chunk)]
        copies += [send(got, got, on_y(o)) for o in (2, 1, 3)]

    def gather_end(state):
        for c in state[3]:
            c.wait_recv()

    def gate_up(h, z):
        four = jnp.concatenate([b.nt[k, z].reshape(SW, 128) for k in range(4)], axis=1)
        for w, put in ((b.wg, 0), (b.wu, 1)):
            r = dot(w[...], four, NN).astype(BF16)
            for k in range(4):
                lanes = slice(128 * k, 128 * (k + 1))
                b.g1[h, k, put * HALF : (put + 1) * HALF] = r[:HALF, lanes]
                low = 2 * HALF + put * (HW - HALF)
                b.g1[h, k, low : low + HW - HALF] = r[HALF:, lanes]

    spread_forward(near)
    spread_end(near)
    gate_up(1, zh)
    spread_forward(far)
    t1 = []
    for o in range(1, 8):
        k = (s + o) % 8
        t1.append(send(b.u.at[k], b.t1r.at[s], {"section": k}))
    spread_end(far)
    gate_up(0, far_z)
    far_rows = [reduce_send(b.g1, b.gr, 0, chunk) for chunk in BOTH]
    near_rows = [reduce_send(b.g1, b.gr, 1, chunk) for chunk in BOTH]
    stores = [pltpu.make_async_copy(b.nt, outs[0], out_sem.at[0])]
    stores[0].start()
    across = [reduce_across(far_rows[0], b.g1, b.gr, b.gzs, b.gzr, BOTH[0])]

    for c in t1:
        c.wait_recv()
    for k in range(4):
        cut = slice(k * (TW // 4), (k + 1) * (TW // 4))
        acc = b.u[s, :, cut].astype(F32)
        for o in range(1, 8):
            acc = acc + b.t1r[(s + o) % 8, :, cut].astype(F32)
        b.pk[s, :, cut] = acc.astype(BF16)
    t2 = spread_start(lambda k: b.pk.at[k])
    across.append(reduce_across(far_rows[1], b.g1, b.gr, b.gzs, b.gzr, BOTH[1]))

    hidden = []
    for n in range(2):
        for c in near_rows[n]:
            c.wait_recv()
        across[n].wait_recv()
        low, mid, high = BOTH[n][0], (BOTH[n][0] + BOTH[n][1]) // 2, BOTH[n][1]
        gate = partial_sum(b.g1, b.gr, 1, low, mid) + b.gzr[low:mid].astype(F32)
        up = partial_sum(b.g1, b.gr, 1, mid, high) + b.gzr[mid:high].astype(F32)
        sig = 1.0 / (1.0 + jnp.exp(-gate))
        b.ht[y, zh, HIDDEN[n][0] : HIDDEN[n][1]] = (gate * sig * up).astype(BF16)
        hidden.append(gather_start(b.ht, HIDDEN[n]))
        b.aa[y, zh, low:mid] = (up * sig * (1.0 + gate * (1.0 - sig))).astype(BF16)
        b.aa[y, zh, mid:high] = (gate * sig).astype(BF16)
    gather_forward(hidden[0])
    spread_forward(t2)
    gather_forward(hidden[1])
    own_factors = b.aa.at[y, zh]
    far_factors = send(own_factors, own_factors, other_z)

    spread_end(t2)
    squares = jnp.zeros((128, 1), F32)
    for k in range(4):
        v = b.pk[:, :, k * (TW // 4) : (k + 1) * (TW // 4)].reshape(128, TW // 4).astype(F32)
        squares = squares + jnp.sum(v * v, axis=1, keepdims=True)
    squares = jnp.broadcast_to(squares, (128, 128))
    high = squares.astype(BF16)
    b.prs[:, :, SW : SW + 128] = high.reshape(4, 32, 128)
    b.prs[:, :, SW + 128 :] = (squares - high.astype(F32)).astype(BF16).reshape(4, 32, 128)
    loads["proj"].wait()
    b.prs[:, :, :SW] = dot(b.pk[...].reshape(128, TW), b.projv[...], NN).astype(BF16).reshape(4, 32, SW)
    t3 = [send(b.prs.at[(t + o) % 4], b.t3r.at[o - 1], on_tp(o)) for o in range(1, 4)]
    loads["wd"].wait()
    for n in range(2):
        gather_end(hidden[n])

    pb, d1r, q = (b.pb0, b.pb1), (b.d1r0, b.d1r1), (b.q0, b.q1)
    d2r, r, d3r, dl = (b.d2r0, b.d2r1), (b.r0, b.r1), (b.d3r0, b.d3r1), (b.dl0, b.dl1)
    factors = (b.aa, (0, 2 * HW), far_factors, [send(own_factors, own_factors, on_y(o)) for o in (2, 1, 3)])
    units = jnp.concatenate([b.ht[k // 2, k % 2] for k in range(8)], axis=1)
    d1 = []
    for n, (low, high) in enumerate(COLUMNS):
        m = dot(units, b.wd[:, low:high], TN).astype(BF16)
        pb[n][...] = m.reshape(8, 4, 2, 16, high - low)
        d1.append(send(pb[n].at[:, :, 1 - core], d1r[n], other_core))
    d2 = []
    for n in range(2):
        d1[n].wait_recv()
        for k in range(8):
            q[n][k] = (pb[n][k, :, core].astype(F32) + d1r[n][k].astype(F32)).astype(BF16)
        d2.append([send(q[n].at[:, (x + o) % 4], d2r[n].at[o - 1], on_x(o)) for o in (2, 1, 3)])

    for c in t3:
        c.wait_recv()
    acc = b.prs[t].astype(F32)
    for o in range(3):
        acc = acc + b.t3r[o].astype(F32)
    squares = acc[:, SW : SW + 1] + acc[:, SW + 128 : SW + 129]
    b.t4s[...] = (acc[:, :SW] * lax.rsqrt(squares / TEACHER_WIDTH + EPS)).astype(BF16)
    t4 = describe(b.t4s, b.t4r, swapped)

    @pl.when(s != f)
    def _():
        t4.start()

    @pl.when(s == f)
    def _():
        b.t4r[...] = b.t4s[...]

    gather_forward(factors)
    d3 = []
    for n in range(2):
        for c in d2[n]:
            c.wait_recv()
        for k in range(8):
            acc = q[n][k, x].astype(F32)
            for o in range(3):
                acc = acc + d2r[n][o, k].astype(F32)
            r[n][k // 2, k % 2] = acc.astype(BF16)
        d3.append([send(r[n].at[(t + o) % 4], d3r[n].at[o - 1], on_tp(o)) for o in range(1, 4)])

    @pl.when(s != f)
    def _():
        t4.wait_recv()

    for e in range(2):

        @pl.when(f != 2 * t + e)
        def _():
            describe(b.xr.at[e], b.xr.at[e], {"fsdp": (f + 1) % 8}, e).wait_recv()

    e1 = []
    for n, (low, high) in enumerate(COLUMNS):
        for c in d3[n]:
            c.wait_recv()
        for e in range(2):
            acc = r[n][t, e].astype(F32)
            for o in range(3):
                acc = acc + d3r[n][o, e].astype(F32)
            error = b.xr[e, :, low:high].astype(F32) + acc - b.t4r[e * 16 : (e + 1) * 16, low:high].astype(F32)
            dl[n][2 * t + e, s] = (error / ROWS).astype(BF16)
        own = dl[n].at[pl.ds(2 * t, 2), s]
        e1.append([send(own, own, on_tp(o)) for o in range(1, 4)])
    e2 = []
    for n in range(2):
        for c in e1[n]:
            c.wait_recv()
        e2.append(spread_start(lambda k, buf=dl[n]: buf.at[:, k]))

    def d_hidden(n, z):
        low, high = COLUMNS[n]
        four = jnp.concatenate([dl[n][2 * k + z].reshape(128, high - low) for k in range(4)], axis=0)
        return dot(b.wd[:, low:high], four, NT)

    spread_forward(e2[0])
    spread_end(e2[0])
    b.hacc[0] = d_hidden(0, far_z)
    b.hacc[1] = d_hidden(0, zh)
    spread_forward(e2[1])
    spread_end(e2[1])
    copies = []
    for h, z in ((0, far_z), (1, zh)):
        m = (b.hacc[h] + d_hidden(1, z)).astype(BF16)
        for k in range(4):
            b.h1[h, k] = m[:, 128 * k : 128 * (k + 1)]
        copies.append([reduce_send(b.h1, b.hr, h, chunk) for chunk in HIDDEN])
    gather_end(factors)
    stores.append(pltpu.make_async_copy(b.aa, outs[2], out_sem.at[2]))
    stores[-1].start()
    across = [reduce_across(copies[0][n], b.h1, b.hr, b.hzs, b.hzr, HIDDEN[n]) for n in range(2)]

    units = jnp.concatenate([b.ht[k // 2, k % 2] for k in range(8)], axis=1)
    for n, (low, high) in enumerate(COLUMNS):
        b.down[:, low:high] = dot(units, dl[n][...].reshape(1024, high - low), NN)
    stores.append(pltpu.make_async_copy(b.down, outs[1], out_sem.at[1]))
    stores[-1].start()
    last = []
    for n, (low, high) in enumerate(HIDDEN):
        for c in copies[1][n]:
            c.wait_recv()
        across[n].wait_recv()
        b.dh[y, zh, low:high] = (partial_sum(b.h1, b.hr, 1, low, high) + b.hzr[low:high].astype(F32)).astype(BF16)
        last.append(gather_start(b.dh, HIDDEN[n]))
    for n in range(2):
        gather_forward(last[n])
    for n in range(2):
        gather_end(last[n])
        part = rows_of(HIDDEN[n])
        stores.append(pltpu.make_async_copy(b.dh.at[:, :, part], outs[3].at[:, :, part], out_sem.at[3 + n]))
        stores[-1].start()

    for c in started:
        c.wait_send()

    @pl.when(s != f)
    def _():
        t4.wait_send()

    @pl.when(y == t)
    def _():
        for c in xsends:
            c.wait_send()

    for c in stores:
        c.wait()
    assert used[0] <= N_SEM


def gradients(nt, down, aa, dh, gate_o, up_o, down_o, nt_v, aa_v, dh_v, grad_v, down_v, sems):
    loads = [
        pltpu.make_async_copy(src, dst, sems.at[k])
        for k, (src, dst) in enumerate(((dh, dh_v), (aa, aa_v), (nt, nt_v), (down, down_v)))
    ]
    for c in loads:
        c.start()
    loads[0].wait()
    loads[1].wait()

    def hidden_grad(put):
        parts = []
        for n in range(2):
            (low, high), (first, last) = HIDDEN[n], BOTH[n]
            rows = slice(first + put * (high - low), first + (put + 1) * (high - low))
            parts.append(
                jnp.concatenate(
                    [(dh_v[k, low:high].astype(F32) * aa_v[k, rows].astype(F32)).astype(BF16) for k in range(8)],
                    axis=1,
                )
            )
        return jnp.concatenate(parts, axis=0)

    d_gate, d_up = hidden_grad(0), hidden_grad(1)
    loads[3].wait()
    down_store = pltpu.make_async_copy(down_v, down_o, sems.at[6])
    down_store.start()
    loads[2].wait()
    normed = jnp.concatenate([nt_v[k] for k in range(8)], axis=1)
    grad_v[0] = dot(d_gate, normed, NT)
    gate_store = pltpu.make_async_copy(grad_v.at[0], gate_o, sems.at[4])
    gate_store.start()
    grad_v[1] = dot(d_up, normed, NT)
    up_store = pltpu.make_async_copy(grad_v.at[1], up_o, sems.at[5])
    up_store.start()
    down_store.wait()
    gate_store.wait()
    up_store.wait()


def on_device(
    teacher_updates, layer_map, route, projector, student_in, norm_gain, w_gate, w_up, w_down
):
    vmem = pl.BlockSpec(memory_space=pltpu.VMEM)
    hbm = pl.BlockSpec(memory_space=pl.ANY)
    nt, down, aa, dh = pl.pallas_call(
        kernel,
        out_shape=[jax.ShapeDtypeStruct(*out) for out in OUTS],
        in_specs=[hbm, vmem, vmem, hbm, vmem, vmem, hbm, hbm, hbm],
        out_specs=[hbm] * len(OUTS),
        scratch_shapes=[pltpu.VMEM(shape, kind) for _, shape, kind in SCRATCH]
        + [pltpu.SemaphoreType.DMA((n,)) for n in (N_SEM, N_SEM, 5, 5)],
        compiler_params=pltpu.CompilerParams(
            collective_id=0, has_side_effects=True, vmem_limit_bytes=56 * 1024 * 1024
        ),
    )(
        teacher_updates.reshape(32, 4, TW),
        layer_map,
        route,
        projector,
        student_in.reshape(8, 16, STUDENT_WIDTH),
        norm_gain.reshape(1, STUDENT_WIDTH),
        w_gate.T,
        w_up.T,
        w_down,
    )

    gate_grad, up_grad, down_grad = pl.pallas_call(
        gradients,
        out_shape=[jax.ShapeDtypeStruct((HW, SW), F32)] * 3,
        in_specs=[hbm] * 4,
        out_specs=[hbm] * 3,
        scratch_shapes=[
            pltpu.VMEM((8, SW, 128), BF16),
            pltpu.VMEM((8, 2 * HW, 128), BF16),
            pltpu.VMEM((8, HW, 128), BF16),
            pltpu.VMEM((2, HW, SW), F32),
            pltpu.VMEM((HW, SW), F32),
            pltpu.SemaphoreType.DMA((7,)),
        ],
        compiler_params=pltpu.CompilerParams(vmem_limit_bytes=56 * 1024 * 1024),
    )(nt.reshape(8, SW, 128), down, aa.reshape(8, 2 * HW, 128), dh.reshape(8, HW, 128))
    return gate_grad.T, up_grad.T, down_grad


def solution(mesh):
    placed = (
        P("section", "fsdp", None, "tp"),
        P(),
        P(),
        P("tp", "section"),
        P("fsdp", None, None, None),
        P(),
        P("fsdp", ("section", "tp")),
        P("fsdp", ("section", "tp")),
        P(("section", "tp"), "fsdp"),
    )
    return jax.shard_map(
        on_device,
        mesh=mesh,
        in_specs=placed,
        out_specs=(
            P("fsdp", ("section", "tp")),
            P("fsdp", ("section", "tp")),
            P(("section", "tp"), "fsdp"),
        ),
        check_vma=False,
    )
```

```python
import jax
import jax.numpy as jnp
from jax import lax
from jax.experimental import pallas as pl
from jax.experimental.pallas import tpu as pltpu
from jax.sharding import PartitionSpec as P

MESH = pl.DeviceIdType.MESH
EPS = 1e-05
F32 = jnp.float32
BF16 = jnp.bfloat16

TW = 4096
SW = 640
SUB = 80
HW = 400
TEACHER_WIDTH = 16384
STUDENT_WIDTH = 5120
ROWS = 4

NN = (((1,), (0,)), ((), ()))
NT = (((1,), (1,)), ((), ()))
TN = (((0,), (0,)), ((), ()))


def dot(a, b, dims):
    return lax.dot_general(a, b, dims, preferred_element_type=F32)


SCRATCH = (
    ("updv", (32, 4, TW), BF16),
    ("projv", (TW, SW), BF16),
    ("wg", (HW, SW), BF16),
    ("wu", (HW, SW), BF16),
    ("wd", (HW, SW), BF16),
    ("u", (8, 16, TW), BF16),
    ("t1r", (8, 16, TW), BF16),
    ("pk", (8, 16, TW), BF16),
    ("prs", (4, 32, SW + 256), BF16),
    ("t3r", (3, 32, SW + 256), BF16),
    ("t4s", (32, SW), BF16),
    ("t4r", (32, SW), BF16),
    ("xr", (2, 16, SW), BF16),
    ("a1s", (7, SUB, 128), BF16),
    ("nt", (4, 2, 8, SUB, 128), BF16),
    ("g1", (2, 4, 2 * HW, 128), BF16),
    ("gr", (2, 3, 2 * HW, 128), BF16),
    ("gzs", (2 * HW, 128), BF16),
    ("gzr", (2 * HW, 128), BF16),
    ("aa", (4, 2, 2 * HW, 128), BF16),
    ("ht", (4, 2, HW, 128), BF16),
    ("pb0", (8, 4, 2, 16, 384), BF16),
    ("d1r0", (8, 4, 16, 384), BF16),
    ("q0", (8, 4, 16, 384), BF16),
    ("d2r0", (3, 8, 16, 384), BF16),
    ("r0", (4, 2, 16, 384), BF16),
    ("d3r0", (3, 2, 16, 384), BF16),
    ("dl0", (8, 8, 16, 384), BF16),
    ("pb1", (8, 4, 2, 16, 256), BF16),
    ("d1r1", (8, 4, 16, 256), BF16),
    ("q1", (8, 4, 16, 256), BF16),
    ("d2r1", (3, 8, 16, 256), BF16),
    ("r1", (4, 2, 16, 256), BF16),
    ("d3r1", (3, 2, 16, 256), BF16),
    ("dl1", (8, 8, 16, 256), BF16),
    ("hacc", (2, HW, 512), F32),
    ("down", (HW, SW), F32),
    ("h1", (2, 4, HW, 128), BF16),
    ("hr", (2, 3, HW, 128), BF16),
    ("hzs", (HW, 128), BF16),
    ("hzr", (HW, 128), BF16),
    ("dh", (4, 2, HW, 128), BF16),
)
N_SEM = 192
OUTS = (
    ((4, 2, 8, SUB, 128), BF16),
    ((HW, SW), F32),
    ((4, 2, 2 * HW, 128), BF16),
    ((4, 2, HW, 128), BF16),
)
HALF = 208
HIDDEN = ((0, HALF), (HALF, HW))
BOTH = ((0, 2 * HALF), (2 * HALF, 2 * HW))
COLUMNS = ((0, 384), (384, SW))


class Refs:
    pass


def selection(layer_map, route, f, s):
    lane = lax.broadcasted_iota(jnp.int32, (32, 128), 1)
    slot = lax.broadcasted_iota(jnp.int32, (32, 128), 0)
    widen = jnp.where(lane // ROWS == slot, 1.0, 0.0).astype(BF16)
    mine = lax.broadcasted_iota(jnp.int32, (8, 128), 0) == f

    def row(table):
        wide = dot(table[...].astype(F32).astype(BF16), widen, NN)
        return jnp.sum(jnp.where(mine, wide, 0.0), axis=0, keepdims=True)

    dest, layer = row(route), row(layer_map)
    across = jnp.broadcast_to(dest, (128, 128))
    a = lax.broadcasted_iota(jnp.int32, (128, 128), 0)
    c = lax.broadcasted_iota(jnp.int32, (128, 128), 1)
    earlier = (across.T == across) & (a // ROWS < c // ROWS) & (a % ROWS == 0)
    rank = jnp.sum(jnp.where(earlier, 1.0, 0.0), axis=0, keepdims=True)
    place = (dest * 4.0 + rank) * ROWS + (c[0:1] % ROWS).astype(F32)
    place = jnp.where(layer >= s.astype(F32), place, -1.0)
    return jnp.where(a.astype(F32) == place, 1.0, 0.0).astype(BF16)


def kernel(upd, layer_map, route, proj, xin, gain, wg, wu, wd, *rest):
    outs, scratch = rest[: len(OUTS)], rest[len(OUTS) :]
    b = Refs()
    for (name, _, _), ref in zip(SCRATCH, scratch):
        setattr(b, name, ref)
    send_sem, recv_sem, in_sem, out_sem = scratch[len(SCRATCH) :]
    s = lax.axis_index("section")
    t = lax.axis_index("tp")
    f = lax.axis_index("fsdp")
    x, core = s // 2, s % 2
    y, zh = f // 2, f % 2
    far_z = 1 - zh
    used = [2]
    started = []

    def describe(src, dst, dev, sem=None):
        if sem is None:
            sem = used[0]
            used[0] += 1
        return pltpu.make_async_remote_copy(
            src_ref=src,
            dst_ref=dst,
            send_sem=send_sem.at[sem],
            recv_sem=recv_sem.at[sem],
            device_id=dev,
            device_id_type=MESH,
        )

    def send(src, dst, dev):
        copy = describe(src, dst, dev)
        copy.start()
        started.append(copy)
        return copy

    def on_x(o):
        return {"section": (x + o) % 4 * 2 + core}

    def on_y(o):
        return {"fsdp": (y + o) % 4 * 2 + zh}

    def on_tp(o):
        return {"tp": (t + o) % 4}

    other_core = {"section": x * 2 + 1 - core}
    other_z = {"fsdp": y * 2 + far_z}
    swapped = {"section": f, "fsdp": s}

    barrier = pltpu.get_barrier_semaphore()
    for o in range(1, 8):
        pl.semaphore_signal(barrier, inc=1, device_id={"section": (s + o) % 8}, device_id_type=MESH)
        pl.semaphore_signal(barrier, inc=1, device_id={"fsdp": (f + o) % 8}, device_id_type=MESH)
    for o in range(1, 4):
        pl.semaphore_signal(barrier, inc=1, device_id=on_tp(o), device_id_type=MESH)

    @pl.when(s != f)
    def _():
        pl.semaphore_signal(barrier, inc=1, device_id=swapped, device_id_type=MESH)

    loads = {}
    for k, (name, src, dst) in enumerate(
        (("wg", wg, b.wg), ("wu", wu, b.wu), ("upd", upd, b.updv), ("proj", proj, b.projv), ("wd", wd, b.wd))
    ):
        loads[name] = pltpu.make_async_copy(src, dst, in_sem.at[k])
        loads[name].start()

    def student(k):
        return xin[:, :, k * SW : (k + 1) * SW].reshape(128, SW).astype(F32)

    total = jnp.zeros((128, 128), F32)
    for k in range(8):
        v = student(k)
        for c in range(0, SW, 128):
            total = total + v[:, c : c + 128] * v[:, c : c + 128]
    total = jnp.sum(total, axis=1, keepdims=True)
    inv = lax.rsqrt(total / STUDENT_WIDTH + EPS)
    rows = lax.broadcasted_iota(jnp.int32, (SUB, SW), 0)
    cols = lax.broadcasted_iota(jnp.int32, (SUB, SW), 1)
    sel = jnp.where(cols == rows + s * SUB, 1.0, 0.0).astype(BF16)
    pl.semaphore_wait(barrier, jnp.where(s == f, 17, 18))

    a1 = {}
    order = ((1, 0), (1, 1), (1, 3), (1, 2), (0, 1), (0, 3), (0, 2), (0, 0))
    for n, (dz, dy) in enumerate(order):
        k = (y + dy) % 4 * 2 + (zh + dz) % 2
        lanes = pl.ds(pl.multiple_of(k * SW, 128), SW)
        v = xin[:, :, lanes].reshape(128, SW).astype(F32)
        piece = dot(sel, (v * inv * gain[:, lanes]).astype(BF16), NT).astype(BF16)
        if n < 7:
            b.a1s[n] = piece
            a1[dz, dy] = send(b.a1s.at[n], b.nt.at[y, zh, s], {"fsdp": k})
        else:
            b.nt[y, zh, s] = piece

    xsends = []
    for o in range(1, 8):
        k = (f + o) % 8
        c = pltpu.make_async_remote_copy(
            src_ref=xin.at[s, :, pl.ds(pl.multiple_of(k * SW, 128), SW)],
            dst_ref=b.xr.at[zh],
            send_sem=send_sem.at[used[0]],
            recv_sem=recv_sem.at[zh],
            device_id={"fsdp": k},
            device_id_type=MESH,
        )
        used[0] += 1
        xsends.append(c)

    @pl.when(y == t)
    def _():
        for c in xsends:
            c.start()
        b.xr[zh] = xin[s, :, pl.ds(pl.multiple_of(f * SW, 128), SW)]

    def spread_start(at):
        copies = [send(at(s), at(s), on_x(o)) for o in range(1, 4)]
        across = [send(at(s), at(s), other_core)]
        return at, copies, across

    def spread_forward(state):
        at, copies, across = state
        for o in range(1, 4):
            copies[o - 1].wait_recv()
            k = (x - o + 4) % 4 * 2 + core
            across.append(send(at(k), at(k), other_core))

    def spread_end(state):
        for c in state[2]:
            c.wait_recv()

    for dy in (1, 2, 3):
        a1[0, dy].wait_recv()
    near = spread_start(lambda k: b.nt.at[:, zh, k])

    perm = selection(layer_map, route, f, s)
    loads["upd"].wait()
    for k in range(4):
        cut = slice(k * (TW // 4), (k + 1) * (TW // 4))
        part = b.updv[:, :, cut].reshape(128, TW // 4)
        b.u[:, :, cut] = dot(perm, part, NN).astype(BF16).reshape(8, 16, TW // 4)

    for dy in (0, 1, 2, 3):
        a1[1, dy].wait_recv()
    far = spread_start(lambda k: b.nt.at[:, far_z, k])
    loads["wg"].wait()
    loads["wu"].wait()

    def rows_of(chunk):
        return pl.ds(chunk[0], chunk[1] - chunk[0])

    def reduce_send(src, got, h, chunk):
        part = rows_of(chunk)
        return [send(src.at[h, (y + o) % 4, part], got.at[h, o - 1, part], on_y(o)) for o in (2, 1, 3)]

    def partial_sum(src, got, h, low, high):
        acc = src[h, y, low:high].astype(F32)
        for o in range(3):
            acc = acc + got[h, o, low:high].astype(F32)
        return acc

    def reduce_across(copies, src, got, zs, zr, chunk):
        for c in copies:
            c.wait_recv()
        for k in range(chunk[0], chunk[1], 16 * 13):
            top = min(k + 16 * 13, chunk[1])
            zs[k:top] = partial_sum(src, got, 0, k, top).astype(BF16)
        return send(zs.at[rows_of(chunk)], zr.at[rows_of(chunk)], other_z)

    def gather_start(buf, chunk):
        own = buf.at[y, zh, rows_of(chunk)]
        far = send(own, own, other_z)
        return buf, chunk, far, [send(own, own, on_y(o)) for o in (2, 1, 3)]

    def gather_forward(state):
        buf, chunk, far, copies = state
        far.wait_recv()
        got = buf.at[y, far_z, rows_of(chunk)]
        copies += [send(got, got, on_y(o)) for o in (2, 1, 3)]

    def gather_end(state):
        for c in state[3]:
            c.wait_recv()

    def gate_up(h, z):
        four = jnp.concatenate([b.nt[k, z].reshape(SW, 128) for k in range(4)], axis=1)
        sent = []
        for (first, last), (top, end) in zip(HIDDEN, BOTH):
            for put, w in enumerate((b.wg, b.wu)):
                m = dot(w[first:last], four, NN).astype(BF16)
                low = top + put * (last - first)
                for k in range(4):
                    b.g1[h, k, low : low + last - first] = m[:, 128 * k : 128 * (k + 1)]
            if h == 0:
                sent.append(reduce_send(b.g1, b.gr, h, (top, end)))
        return sent

    spread_forward(near)
    spread_end(near)
    gate_up(1, zh)
    spread_forward(far)
    t1 = []
    for o in range(1, 8):
        k = (s + o) % 8
        t1.append(send(b.u.at[k], b.t1r.at[s], {"section": k}))
    spread_end(far)
    far_rows = gate_up(0, far_z)
    near_rows = [reduce_send(b.g1, b.gr, 1, chunk) for chunk in BOTH]
    stores = [pltpu.make_async_copy(b.nt, outs[0], out_sem.at[0])]
    stores[0].start()
    across = [reduce_across(far_rows[0], b.g1, b.gr, b.gzs, b.gzr, BOTH[0])]

    for c in t1:
        c.wait_recv()
    for k in range(4):
        cut = slice(k * (TW // 4), (k + 1) * (TW // 4))
        acc = b.u[s, :, cut].astype(F32)
        for o in range(1, 8):
            acc = acc + b.t1r[(s + o) % 8, :, cut].astype(F32)
        b.pk[s, :, cut] = acc.astype(BF16)
    t2 = spread_start(lambda k: b.pk.at[k])
    across.append(reduce_across(far_rows[1], b.g1, b.gr, b.gzs, b.gzr, BOTH[1]))

    hidden = []
    for n in range(2):
        for c in near_rows[n]:
            c.wait_recv()
        across[n].wait_recv()
        low, mid, high = BOTH[n][0], (BOTH[n][0] + BOTH[n][1]) // 2, BOTH[n][1]
        gate = partial_sum(b.g1, b.gr, 1, low, mid) + b.gzr[low:mid].astype(F32)
        up = partial_sum(b.g1, b.gr, 1, mid, high) + b.gzr[mid:high].astype(F32)
        sig = 1.0 / (1.0 + jnp.exp(-gate))
        b.ht[y, zh, HIDDEN[n][0] : HIDDEN[n][1]] = (gate * sig * up).astype(BF16)
        hidden.append(gather_start(b.ht, HIDDEN[n]))
        b.aa[y, zh, low:mid] = (up * sig * (1.0 + gate * (1.0 - sig))).astype(BF16)
        b.aa[y, zh, mid:high] = (gate * sig).astype(BF16)
    gather_forward(hidden[0])
    spread_forward(t2)
    gather_forward(hidden[1])
    own_factors = b.aa.at[y, zh]
    far_factors = send(own_factors, own_factors, other_z)

    spread_end(t2)
    squares = jnp.zeros((128, 1), F32)
    for k in range(4):
        v = b.pk[:, :, k * (TW // 4) : (k + 1) * (TW // 4)].reshape(128, TW // 4).astype(F32)
        squares = squares + jnp.sum(v * v, axis=1, keepdims=True)
    squares = jnp.broadcast_to(squares, (128, 128))
    high = squares.astype(BF16)
    b.prs[:, :, SW : SW + 128] = high.reshape(4, 32, 128)
    b.prs[:, :, SW + 128 :] = (squares - high.astype(F32)).astype(BF16).reshape(4, 32, 128)
    loads["proj"].wait()
    b.prs[:, :, :SW] = dot(b.pk[...].reshape(128, TW), b.projv[...], NN).astype(BF16).reshape(4, 32, SW)
    t3 = [send(b.prs.at[(t + o) % 4], b.t3r.at[o - 1], on_tp(o)) for o in range(1, 4)]
    loads["wd"].wait()
    for n in range(2):
        gather_end(hidden[n])

    pb, d1r, q = (b.pb0, b.pb1), (b.d1r0, b.d1r1), (b.q0, b.q1)
    d2r, r, d3r, dl = (b.d2r0, b.d2r1), (b.r0, b.r1), (b.d3r0, b.d3r1), (b.dl0, b.dl1)
    factors = (b.aa, (0, 2 * HW), far_factors, [send(own_factors, own_factors, on_y(o)) for o in (2, 1, 3)])
    units = jnp.concatenate([b.ht[k // 2, k % 2] for k in range(8)], axis=1)
    d1 = []
    for n, (low, high) in enumerate(COLUMNS):
        m = dot(units, b.wd[:, low:high], TN).astype(BF16)
        pb[n][...] = m.reshape(8, 4, 2, 16, high - low)
        d1.append(send(pb[n].at[:, :, 1 - core], d1r[n], other_core))
    d2 = []
    for n in range(2):
        d1[n].wait_recv()
        for k in range(8):
            q[n][k] = (pb[n][k, :, core].astype(F32) + d1r[n][k].astype(F32)).astype(BF16)
        d2.append([send(q[n].at[:, (x + o) % 4], d2r[n].at[o - 1], on_x(o)) for o in (2, 1, 3)])

    for c in t3:
        c.wait_recv()
    acc = b.prs[t].astype(F32)
    for o in range(3):
        acc = acc + b.t3r[o].astype(F32)
    squares = acc[:, SW : SW + 1] + acc[:, SW + 128 : SW + 129]
    b.t4s[...] = (acc[:, :SW] * lax.rsqrt(squares / TEACHER_WIDTH + EPS)).astype(BF16)
    t4 = describe(b.t4s, b.t4r, swapped)

    @pl.when(s != f)
    def _():
        t4.start()

    @pl.when(s == f)
    def _():
        b.t4r[...] = b.t4s[...]

    gather_forward(factors)
    d3 = []
    for n in range(2):
        for c in d2[n]:
            c.wait_recv()
        for k in range(8):
            acc = q[n][k, x].astype(F32)
            for o in range(3):
                acc = acc + d2r[n][o, k].astype(F32)
            r[n][k // 2, k % 2] = acc.astype(BF16)
        d3.append([send(r[n].at[(t + o) % 4], d3r[n].at[o - 1], on_tp(o)) for o in range(1, 4)])

    @pl.when(s != f)
    def _():
        t4.wait_recv()

    for e in range(2):

        @pl.when(f != 2 * t + e)
        def _():
            describe(b.xr.at[e], b.xr.at[e], {"fsdp": (f + 1) % 8}, e).wait_recv()

    e1 = []
    for n, (low, high) in enumerate(COLUMNS):
        for c in d3[n]:
            c.wait_recv()
        for e in range(2):
            acc = r[n][t, e].astype(F32)
            for o in range(3):
                acc = acc + d3r[n][o, e].astype(F32)
            error = b.xr[e, :, low:high].astype(F32) + acc - b.t4r[e * 16 : (e + 1) * 16, low:high].astype(F32)
            dl[n][2 * t + e, s] = (error / ROWS).astype(BF16)
        own = dl[n].at[pl.ds(2 * t, 2), s]
        e1.append([send(own, own, on_tp(o)) for o in range(1, 4)])
    e2 = []
    for n in range(2):
        for c in e1[n]:
            c.wait_recv()
        e2.append(spread_start(lambda k, buf=dl[n]: buf.at[:, k]))

    def d_hidden(n, z, first=0, last=HW):
        low, high = COLUMNS[n]
        four = jnp.concatenate([dl[n][2 * k + z].reshape(128, high - low) for k in range(4)], axis=0)
        return dot(b.wd[first:last, low:high], four, NT)

    spread_forward(e2[0])
    spread_end(e2[0])
    b.hacc[0] = d_hidden(0, far_z)
    b.hacc[1] = d_hidden(0, zh)
    spread_forward(e2[1])
    spread_end(e2[1])
    copies = []
    for h, z in ((0, far_z), (1, zh)):
        sent = []
        for first, last in HIDDEN:
            m = (b.hacc[h, first:last] + d_hidden(1, z, first, last)).astype(BF16)
            for k in range(4):
                b.h1[h, k, first:last] = m[:, 128 * k : 128 * (k + 1)]
            sent.append(reduce_send(b.h1, b.hr, h, (first, last)))
        copies.append(sent)
    gather_end(factors)
    stores.append(pltpu.make_async_copy(b.aa, outs[2], out_sem.at[2]))
    stores[-1].start()
    across = [reduce_across(copies[0][n], b.h1, b.hr, b.hzs, b.hzr, HIDDEN[n]) for n in range(2)]

    units = jnp.concatenate([b.ht[k // 2, k % 2] for k in range(8)], axis=1)
    for n, (low, high) in enumerate(COLUMNS):
        b.down[:, low:high] = dot(units, dl[n][...].reshape(1024, high - low), NN)
    stores.append(pltpu.make_async_copy(b.down, outs[1], out_sem.at[1]))
    stores[-1].start()
    last = []
    for n, (low, high) in enumerate(HIDDEN):
        for c in copies[1][n]:
            c.wait_recv()
        across[n].wait_recv()
        b.dh[y, zh, low:high] = (partial_sum(b.h1, b.hr, 1, low, high) + b.hzr[low:high].astype(F32)).astype(BF16)
        last.append(gather_start(b.dh, HIDDEN[n]))
    for n in range(2):
        gather_forward(last[n])
    for n in range(2):
        gather_end(last[n])
        part = rows_of(HIDDEN[n])
        stores.append(pltpu.make_async_copy(b.dh.at[:, :, part], outs[3].at[:, :, part], out_sem.at[3 + n]))
        stores[-1].start()

    for c in started:
        c.wait_send()

    @pl.when(s != f)
    def _():
        t4.wait_send()

    @pl.when(y == t)
    def _():
        for c in xsends:
            c.wait_send()

    for c in stores:
        c.wait()
    assert used[0] <= N_SEM


def gradients(nt, down, aa, dh, gate_o, up_o, down_o, nt_v, aa_v, dh_v, grad_v, down_v, sems):
    loads = [
        pltpu.make_async_copy(src, dst, sems.at[k])
        for k, (src, dst) in enumerate(((dh, dh_v), (aa, aa_v), (nt, nt_v), (down, down_v)))
    ]
    for c in loads:
        c.start()
    loads[0].wait()
    loads[1].wait()

    def hidden_grad(put):
        parts = []
        for n in range(2):
            (low, high), (first, last) = HIDDEN[n], BOTH[n]
            rows = slice(first + put * (high - low), first + (put + 1) * (high - low))
            parts.append(
                jnp.concatenate(
                    [(dh_v[k, low:high].astype(F32) * aa_v[k, rows].astype(F32)).astype(BF16) for k in range(8)],
                    axis=1,
                )
            )
        return jnp.concatenate(parts, axis=0)

    d_gate, d_up = hidden_grad(0), hidden_grad(1)
    loads[3].wait()
    down_store = pltpu.make_async_copy(down_v, down_o, sems.at[6])
    down_store.start()
    loads[2].wait()
    normed = jnp.concatenate([nt_v[k] for k in range(8)], axis=1)
    grad_v[0] = dot(d_gate, normed, NT)
    gate_store = pltpu.make_async_copy(grad_v.at[0], gate_o, sems.at[4])
    gate_store.start()
    grad_v[1] = dot(d_up, normed, NT)
    up_store = pltpu.make_async_copy(grad_v.at[1], up_o, sems.at[5])
    up_store.start()
    down_store.wait()
    gate_store.wait()
    up_store.wait()


def on_device(
    teacher_updates, layer_map, route, projector, student_in, norm_gain, w_gate, w_up, w_down
):
    vmem = pl.BlockSpec(memory_space=pltpu.VMEM)
    hbm = pl.BlockSpec(memory_space=pl.ANY)
    nt, down, aa, dh = pl.pallas_call(
        kernel,
        out_shape=[jax.ShapeDtypeStruct(*out) for out in OUTS],
        in_specs=[hbm, vmem, vmem, hbm, vmem, vmem, hbm, hbm, hbm],
        out_specs=[hbm] * len(OUTS),
        scratch_shapes=[pltpu.VMEM(shape, kind) for _, shape, kind in SCRATCH]
        + [pltpu.SemaphoreType.DMA((n,)) for n in (N_SEM, N_SEM, 5, 5)],
        compiler_params=pltpu.CompilerParams(
            collective_id=0, has_side_effects=True, vmem_limit_bytes=56 * 1024 * 1024
        ),
    )(
        teacher_updates.reshape(32, 4, TW),
        layer_map,
        route,
        projector,
        student_in.reshape(8, 16, STUDENT_WIDTH),
        norm_gain.reshape(1, STUDENT_WIDTH),
        w_gate.T,
        w_up.T,
        w_down,
    )

    gate_grad, up_grad, down_grad = pl.pallas_call(
        gradients,
        out_shape=[jax.ShapeDtypeStruct((HW, SW), F32)] * 3,
        in_specs=[hbm] * 4,
        out_specs=[hbm] * 3,
        scratch_shapes=[
            pltpu.VMEM((8, SW, 128), BF16),
            pltpu.VMEM((8, 2 * HW, 128), BF16),
            pltpu.VMEM((8, HW, 128), BF16),
            pltpu.VMEM((2, HW, SW), F32),
            pltpu.VMEM((HW, SW), F32),
            pltpu.SemaphoreType.DMA((7,)),
        ],
        compiler_params=pltpu.CompilerParams(vmem_limit_bytes=56 * 1024 * 1024),
    )(nt.reshape(8, SW, 128), down, aa.reshape(8, 2 * HW, 128), dh.reshape(8, HW, 128))
    return gate_grad.T, up_grad.T, down_grad


def solution(mesh):
    placed = (
        P("section", "fsdp", None, "tp"),
        P(),
        P(),
        P("tp", "section"),
        P("fsdp", None, None, None),
        P(),
        P("fsdp", ("section", "tp")),
        P("fsdp", ("section", "tp")),
        P(("section", "tp"), "fsdp"),
    )
    return jax.shard_map(
        on_device,
        mesh=mesh,
        in_specs=placed,
        out_specs=(
            P("fsdp", ("section", "tp")),
            P("fsdp", ("section", "tp")),
            P(("section", "tp"), "fsdp"),
        ),
        check_vma=False,
    )
```
